256 devices in a mesh: slot: 16 (over y, z_hi), head: 8 (over x, z_lo), blk: 2 (over core).
Axes of the slice: x: 4, y: 4, z: 8 (z_hi: 4, z_lo: 2; z = z_hi * 2 + z_lo), core: 2. Of those that a mesh axis runs over, the one named last changes fastest.
Arguments:
- query_rows: bfloat16 [16, 1024, 5120], P('slot', ('head', 'blk')), may hold values from -140 to 140
- key_rows: bfloat16 [16, 1024, 5120], P('slot', ('head', 'blk')), may hold values from -140 to 140
- value_rows: bfloat16 [16, 1024, 5120], P('slot', ('head', 'blk')), may hold values from -6 to 6
- query_gain: float32 [5120], replicated, may hold values from 0.1 to 1.9
- key_gain: float32 [5120], replicated, may hold values from 0.1 to 1.9
- out_weight: bfloat16 [5120, 5120], P('head', ('slot', 'blk')), may hold values from -0.5 to 0.5
- gate_table: float32 [50, 5120], replicated, may hold values from 0.5 to 3
- lengths: int32 [16], P('slot'), may hold values from 512 to 1024, as said below
- step_index: int32 [16], P('slot'), may hold values from 0 to 49
Outputs:
- attn_branch: bfloat16 [16, 1024, 5120], P('slot', ('head', 'blk'))
The draws below stay inside these ranges and needn't reach their ends.
Inputs may be any that keep to these rules, and one draw needn't show every extreme that they name: `lengths`: some slot has half of 1024 valid tokens and another all 1024.
All inputs are finite; a program needn't handle non-finite values.
Results may differ from the reference program's by a relative error of at most 0.02.
Values may be sent and summed in bfloat16 or wider, within the bound.
A program may use at most 64 MiB of HBM per device.

```python
import math
import jax
import jax.numpy as jnp
from jax import lax

D = 5120
HEADS = 40
HD = 128
STEPS = 50
SEQ = 1024
SLOTS = 16
N_HEAD = 8


def draw_query_rows(key, part):
    key = jax.random.fold_in(key, 1)
    values = jax.random.truncated_normal(key, -6.0, 6.0, (SLOTS, SEQ, D), jnp.float32)
    return values.astype(jnp.bfloat16)


def draw_key_rows(key, part):
    key = jax.random.fold_in(key, 2)
    values = jax.random.truncated_normal(key, -6.0, 6.0, (SLOTS, SEQ, D), jnp.float32)
    return values.astype(jnp.bfloat16)


def draw_lengths(key, part):
    key = jax.random.fold_in(key, 3)
    first_key, second_key, third_key = jax.random.split(key, 3)
    drawn = jax.random.randint(first_key, (SLOTS,), SEQ // 2, SEQ + 1, dtype=jnp.int32)
    lowest = jax.random.randint(second_key, (), 0, SLOTS, dtype=jnp.int32)
    highest = (lowest + 1 + jax.random.randint(third_key, (), 0, SLOTS - 1, dtype=jnp.int32)) % SLOTS
    slot_ids = jnp.arange(SLOTS, dtype=jnp.int32)
    drawn = jnp.where(slot_ids == lowest, SEQ // 2, drawn)
    drawn = jnp.where(slot_ids == highest, SEQ, drawn)
    return drawn.astype(jnp.int32)


def plant(array, key, smallest, top_value):
    longest = array.shape.index(max(array.shape))
    spots = []
    for shift in (0, 1):
        where = [jax.random.randint(jax.random.fold_in(key, axis), (), 0, length) for axis, length in enumerate(array.shape)]
        where[longest] = (where[longest] + shift) % array.shape[longest]
        spots.append(tuple(where))
    return array.at[spots[0]].set(smallest).at[spots[1]].set(top_value)


def block_scale(key, dims, cuts, least, top_value):
    factor_of = 1.0
    for dim, blocks in cuts:
        heights = jax.random.uniform(jax.random.fold_in(jax.random.fold_in(key, 6), dim), (blocks,), jnp.float32, least / len(cuts), top_value / len(cuts))
        factor_of = factor_of * jnp.repeat(jnp.exp(heights), dims[dim] // blocks).reshape((-1,) + (1,) * (len(dims) - 1 - dim))
    return factor_of


def bell_draw(own_key, extent, deviation, most, cuts=(), kind=jnp.bfloat16):
    gain = block_scale(own_key, extent, cuts, -0.22, 0.18) if cuts else 1.0
    result = jax.random.normal(own_key, extent, jnp.float32) * deviation * gain
    return jnp.minimum(jnp.maximum(result, -most), most).astype(kind)


def setup_inputs(seed: int = 0) -> dict:
    streams_of = jax.random.split(jax.random.key(seed), 10)
    query_rows = draw_query_rows(jax.random.fold_in(streams_of[9], 71), 0)
    key_rows = draw_key_rows(jax.random.fold_in(streams_of[9], 71), 0)
    value_rows = bell_draw(streams_of[2], (SLOTS, SEQ, D), 1.0, 6.0, ((0, 16), (1, 16)))
    query_gain = jnp.clip(1.0 + 0.18 * jax.random.normal(streams_of[3], (D,), jnp.float32), 0.1, 1.9)
    key_gain = jnp.clip(1.0 + 0.18 * jax.random.normal(streams_of[4], (D,), jnp.float32), 0.1, 1.9)
    out_weight = bell_draw(streams_of[5], (D, D), HD ** -0.5, 0.5, ((0, 8), (1, 32)))
    gate_table = jnp.clip(jax.random.uniform(streams_of[6], (STEPS, D), jnp.float32, 0.5, 3.0), 0.5, 3.0)
    lengths = draw_lengths(jax.random.fold_in(streams_of[9], 71), 0)
    step_index = plant(jax.random.randint(streams_of[8], (SLOTS,), 0, STEPS), jax.random.fold_in(streams_of[8], 1), 0, STEPS - 1).astype(jnp.int32)
    return dict(query_rows=query_rows, key_rows=key_rows, value_rows=value_rows, query_gain=query_gain, key_gain=key_gain, out_weight=out_weight, gate_table=gate_table, lengths=lengths, step_index=step_index)


NEG_BIG = -1e+30
EPSILON = 1e-06

def rms_scaled(activations, gain_row):
    values = activations.astype(jnp.float32)
    mean_square = lax.optimization_barrier(jnp.mean(values * values, axis=-1, keepdims=True))
    return (values * lax.rsqrt(mean_square + EPSILON) * gain_row).astype(jnp.bfloat16)

def reference(query_rows, key_rows, value_rows, query_gain, key_gain, out_weight, gate_table, lengths, step_index):
    positions = jnp.arange(SEQ, dtype=jnp.int32)
    group_width = HEADS // N_HEAD * HD

    def one_slot(slot_items):
        slot_queries, slot_keys, slot_values, slot_length, slot_step = slot_items
        query_norm = rms_scaled(slot_queries, query_gain)
        key_norm = rms_scaled(slot_keys, key_gain)
        is_valid = positions < slot_length
        query_heads = query_norm.reshape(SEQ, HEADS, HD).transpose(1, 0, 2)
        key_heads = key_norm.reshape(SEQ, HEADS, HD).transpose(1, 0, 2)
        value_heads = slot_values.reshape(SEQ, HEADS, HD).transpose(1, 0, 2)

        def one_head(head_items):
            head_query, head_key, head_value = head_items
            scores = jnp.dot(head_query, head_key.T, preferred_element_type=jnp.float32)
            scores = scores * (1.0 / math.sqrt(HD))
            scores = jnp.where(is_valid[None, :], scores, NEG_BIG)
            largest = lax.optimization_barrier(jnp.max(scores, axis=1))
            weights = jnp.where(is_valid[None, :], jnp.exp(scores - largest[:, None]), 0.0)
            totals = lax.optimization_barrier(jnp.sum(weights, axis=1))
            mixed = jnp.dot(weights.astype(jnp.bfloat16), head_value, preferred_element_type=jnp.float32)
            return (mixed / totals[:, None]).astype(jnp.bfloat16)
        attended = lax.map(one_head, (query_heads, key_heads, value_heads))
        attended = attended.transpose(1, 0, 2).reshape(SEQ, D)
        projected = jnp.zeros((SEQ, D), jnp.float32)
        for group in range(N_HEAD):
            lower = group * group_width
            upper = lower + group_width
            partial_term = jnp.dot(attended[:, lower:upper], out_weight[lower:upper, :], preferred_element_type=jnp.float32)
            projected = projected + partial_term.astype(jnp.bfloat16).astype(jnp.float32)
        step_rows = jnp.arange(STEPS, dtype=jnp.int32)[:, None]
        gate_row = lax.optimization_barrier(jnp.sum(jnp.where(step_rows == slot_step, gate_table, 0.0), axis=0))
        return (gate_row * projected).astype(jnp.bfloat16)
    return lax.map(one_slot, (query_rows, key_rows, value_rows, lengths, step_index))
```

```python
import functools
import math

import jax
import jax.numpy as jnp
from jax import lax
from jax.experimental import pallas as pl
from jax.experimental.pallas import tpu as pltpu
from jax.sharding import PartitionSpec as P

HD = 128
NEG_BIG = -1e30
EPSILON = 1e-06
MESH = pl.DeviceIdType.MESH

NX, NY, NZ, NC = 4, 4, 8, 2
TOK = 64
D = 5120
GW = 640
LOCAL_HEADS = GW // HD
KEYS = 1024
WC = 160
GC = 2 * WC
GROUPS = 8
STEPS = 50
BF = jnp.bfloat16
F32 = jnp.float32


def al(value, unit):
    return pl.multiple_of(value, unit)


def kernel(
    len_ref, step_ref, q_hbm, k_hbm, v_hbm, qg_ref, kg_ref, w_hbm, gt_hbm, out_hbm,
    q_raw, k_raw, q_nrm, k_nrm, w_raw, w_own, gate_tab, gate_row, qb, kb, vb, bias, wt,
    a_stage, at, pf, far_out, far_in, near_out, near_in, ft, ob,
    ld, qs, qr, ks, kr, vs, vr, fs, fr, w0s, w0r, zs, zr, yds, ydr, yrs, yrr,
    azs, azr, aos, aor, afs, afr, ffs, ffr, nns, nnr, fins, finr, finl,
):
    slot = lax.axis_index("slot")
    head = lax.axis_index("head")
    c = lax.axis_index("blk")
    x, zl = head // 2, head % 2
    y, zh = slot // 4, slot % 4
    z = zh * 2 + zl
    oc = 1 - c
    row_core = y // 2
    is_row_core = c == row_core

    def dev(dx, dy, dz, dc):
        return (dy * 4 + dz // 2, dx * 2 + dz % 2, dc)

    def rc(src, dst, send, recv, device):
        return pltpu.make_async_remote_copy(
            src_ref=src, dst_ref=dst, send_sem=send, recv_sem=recv,
            device_id=device, device_id_type=MESH,
        )

    def got(ref, sem):
        pltpu.make_async_copy(ref, ref, sem).wait()

    xp, xm = (x + 1) % NX, (x + 3) % NX
    yp, ym = (y + 1) % NY, (y + 3) % NY
    zp, zm = (z + 1) % NZ, (z + 7) % NZ
    z_mate = zh * 2 + (1 - zl)
    z_out = (z + NZ - 1 + 2 * zl) % NZ
    other = dev(x, y, z, oc)

    load_w = pltpu.make_async_copy(w_hbm, w_raw, ld.at[0])
    load_k = pltpu.make_async_copy(k_hbm.at[0], k_raw, ld.at[1])
    load_q = pltpu.make_async_copy(q_hbm.at[0], q_raw, ld.at[2])
    load_g = pltpu.make_async_copy(
        gt_hbm.at[:, pl.ds(al(c * 2560, 128), 2560)], gate_tab, ld.at[3]
    )
    load_w.start()
    load_k.start()
    load_q.start()
    load_g.start()

    barrier = pltpu.get_barrier_semaphore()
    partners = []
    for dh in range(8):
        for dc in range(2):
            if (dh, dc) != (0, 0):
                ph = (head + dh) % 8
                partners.append((slot, ph, (c + dc) % 2))
    for dc in range(2):
        partners.append(dev(x, y, z_out, dc))
        partners.append(dev(x, yp, z, dc))
        partners.append(dev(x, ym, z, dc))
    for partner in partners:
        pl.semaphore_signal(barrier, inc=1, device_id=partner, device_id_type=MESH)
    pl.semaphore_wait(barrier, len(partners))

    def cols(ref, group):
        return ref.at[:, pl.ds(al(group * GW, 128), GW)]

    def kv_place(buf, which_c, src_head):
        return buf.at[pl.ds(al(which_c * 512 + src_head * TOK, TOK), TOK), :]

    def kv_send(src, buf, send, recv):
        pltpu.make_async_copy(cols(src, head), kv_place(buf, c, head), recv.at[head]).start()

        def one(t, carry):
            group = (head + t) % 8
            rc(cols(src, group), kv_place(buf, c, head), send.at[group], recv.at[head],
               (slot, group, c)).start()
            return carry
        lax.fori_loop(1, 8, one, 0)

    def kv_send_wait(src, buf, send, recv):
        def one(t, carry):
            group = (head + t) % 8
            rc(cols(src, group), kv_place(buf, c, head), send.at[group], recv.at[head],
               (slot, group, c)).wait_send()
            return carry
        lax.fori_loop(1, 8, one, 0)

    def kv_forward(buf, recv, index):
        def one(t, carry):
            got(kv_place(buf, c, t), recv.at[t])
            return carry
        lax.fori_loop(0, 8, one, 0)
        half = buf.at[pl.ds(al(c * 512, 512), 512), :]
        rc(half, half, fs.at[index], fr.at[index], other).start()

    kv_send(v_hbm.at[0], vb, vs, vr)

    def piece(ys, zs_, half=None):
        row = ((ys % 2) * 4 + zs_ // 2) * GC
        size = GC
        if half is not None:
            row = row + half * WC
            size = WC
        return wt.at[pl.ds(al(row, 32), size), pl.ds(al((zs_ % 2) * GW, 128), GW)]

    load_w.wait()
    w_own[...] = w_raw[...].astype(F32).T.astype(BF)

    @pl.when(is_row_core)
    def _():
        pltpu.make_async_copy(w_own, piece(y, z, c), w0r.at[c]).start()

    @pl.when(jnp.logical_not(is_row_core))
    def _():
        rc(w_own, piece(y, z, c), w0s, w0r.at[c], other).start()

    def row_sends(zsrc, j):
        for d, yt in ((0, yp), (1, ym)):
            yield rc(piece(y, zsrc), piece(y, zsrc), yds.at[d, j], ydr.at[j],
                     dev(x, yt, z, row_core))

    def z_send(d, k):
        zsrc = (z + NZ - (k - 1)) % NZ if d == 0 else (z + k - 1) % NZ
        half = None if k < 4 else d
        return rc(piece(y, zsrc, half), piece(y, zsrc, half), zs.at[d, k - 1], zr.at[d, k - 1],
                  dev(x, y, zp if d == 0 else zm, row_core))

    def z_from(d, k):
        return (z + NZ - k) % NZ if d == 0 else (z + k) % NZ

    def z_index(d, k):
        ahead = zl if d == 0 else 1 - zl
        if k == 1:
            return 2 - ahead
        if k == 2:
            return 3 + ahead
        return 6 - ahead

    def z_first():
        @pl.when(is_row_core)
        def _():
            got(piece(y, z, 0), w0r.at[0])
            got(piece(y, z, 1), w0r.at[1])
            for d in range(2):
                z_send(d, 1).start()
            for cp in row_sends(z, 0):
                cp.start()

    def z_service(k):
        @pl.when(is_row_core)
        def _():
            for d in range(2):
                zsrc = z_from(d, k)
                got(piece(y, zsrc), zr.at[d, k - 1])
                z_send(d, k + 1).start()
                for cp in row_sends(zsrc, z_index(d, k)):
                    cp.start()

    def z_last():
        @pl.when(is_row_core)
        def _():
            zsrc = (z + 4) % NZ
            for d in range(2):
                got(piece(y, zsrc, d), zr.at[d, 3])
            for cp in row_sends(zsrc, 7):
                cp.start()

    from_plus = ((y + 1) % 2) * (1 - (c - row_core) * (c - row_core)) + (y % 2) * (
        (c - row_core) * (c - row_core))
    direct_row = (y + 3 + 2 * from_plus) % NY
    relay_to = (y + 1 + 2 * from_plus) % NY
    sgn = 1 - 2 * zl
    DELTA = (0, 1, -1, -2, 2, 3, -3, 4)

    def z_of(j):
        return (z + NZ + sgn * DELTA[j]) % NZ

    def relay(j):
        zsrc = z_of(j)
        ref = piece(direct_row, zsrc, from_plus)
        return rc(ref, ref, yrs.at[j], yrr.at[from_plus, j], dev(x, relay_to, z, c))

    def y_service(j):
        got(piece(direct_row, z_of(j)), ydr.at[j])
        relay(j).start()

    z_first()

    def norm(raw, gain_ref, out):
        def rows(i, carry):
            here = pl.ds(al(i * 16, 16), 16)
            vals = raw[here, :].astype(F32)
            mean_square = jnp.mean(vals * vals, axis=-1, keepdims=True)
            out[here, :] = (vals * lax.rsqrt(mean_square + EPSILON) * gain_ref[...]).astype(BF)
            return carry
        lax.fori_loop(0, TOK // 16, rows, 0)

    load_k.wait()
    norm(k_raw, kg_ref, k_nrm)
    kv_send(k_nrm, kb, ks, kr)
    load_q.wait()
    norm(q_raw, qg_ref, q_nrm)

    q_core = x // 2

    def q_place(src_x, src_zl, src_c):
        row = src_zl * 256 + (src_x % 2) * 128 + src_c * TOK
        return qb.at[pl.ds(al(row, TOK), TOK), :]

    q_index = (x % 2) * 4 + zl * 2 + c
    q_stays = c == q_core

    @pl.when(q_stays)
    def _():
        pltpu.make_async_copy(cols(q_nrm, head), q_place(x, zl, c), qr.at[q_index]).start()

    def q_copy(group):
        return rc(cols(q_nrm, group), q_place(x, zl, c), qs.at[group], qr.at[q_index],
                  (slot, group, q_core))

    @pl.when(jnp.logical_not(q_stays))
    def _():
        q_copy(head).start()

    def q_send(t, carry):
        q_copy((head + t) % 8).start()
        return carry
    lax.fori_loop(1, 8, q_send, 0)

    def mask_rows(i, carry):
        row = lax.broadcasted_iota(jnp.int32, (TOK, 128), 0)
        pos = (i % 8) * 128 + (i // 8) * TOK + row
        bias[pl.ds(al(i * TOK, TOK), TOK), :] = jnp.where(pos < len_ref[0], 0.0, NEG_BIG)
        return carry
    lax.fori_loop(0, KEYS // TOK, mask_rows, 0)

    load_g.wait()
    step_rows = lax.broadcasted_iota(jnp.int32, (STEPS, 2560), 0)
    gate_row[...] = jnp.sum(
        jnp.where(step_rows == step_ref[0], gate_tab[...], 0.0), axis=0, keepdims=True)

    z_service(1)
    kv_forward(vb, vr, 0)
    y_service(0)
    z_service(2)
    kv_forward(kb, kr, 1)
    y_service(1)
    z_service(3)

    def q_wait(t, carry):
        got(qb.at[pl.ds(al((t // 2 % 2) * 256 + (t // 4) * 128 + (t % 2) * TOK, TOK), TOK), :],
            qr.at[t])
        return carry
    lax.fori_loop(0, 8, q_wait, 0)
    for buf, index in ((vb, 0), (kb, 1)):
        got(buf.at[pl.ds(al(oc * 512, 512), 512), :], fr.at[index])

    scale = math.log2(math.e) / math.sqrt(HD)
    mine = pl.ds(al(c * 256, 128), 256)
    theirs = pl.ds(al(oc * 256, 128), 256)

    def feats(which_zl, hh):
        return pl.ds(al(which_zl * GW + hh * HD, HD), HD)

    def attend(hh, zq):
        lanes = pl.ds(al(hh * HD, HD), HD)
        keys = kb[:, lanes]
        queries = qb[pl.ds(al(zq * 256, 256), 256), lanes]
        scores = lax.dot_general(keys, queries, (((1,), (1,)), ((), ())),
                                 preferred_element_type=F32)
        scores = scores * scale + jnp.concatenate([bias[...], bias[...]], axis=1)
        top = jnp.max(scores, axis=0, keepdims=True)
        weights = jnp.exp2(scores - top)
        total = jnp.sum(weights, axis=0, keepdims=True)
        mixed = lax.dot_general(vb[:, lanes], weights.astype(BF), (((0,), (0,)), ((), ())),
                                preferred_element_type=F32)
        return (mixed / total).astype(BF)

    def away_copy(hh):
        return rc(a_stage.at[hh], at.at[feats(zl, hh), mine], azs.at[hh], azr.at[hh],
                  dev(x, y, z_mate, c))

    def home_copy(hh):
        ref = at.at[feats(zl, hh), mine]
        return rc(ref, ref, aos.at[hh], aor.at[hh], other)

    def pass_copy(hh):
        ref = at.at[feats(1 - zl, hh), mine]
        return rc(ref, ref, afs.at[hh], afr.at[hh], other)

    def one_head(hh, carry):
        a_stage[hh] = attend(hh, 1 - zl)
        away_copy(hh).start()
        at[feats(zl, hh), mine] = attend(hh, zl)
        home_copy(hh).start()
        return carry
    lax.fori_loop(0, 2, one_head, 0)
    y_service(2)
    z_last()
    lax.fori_loop(2, 4, one_head, 0)
    y_service(3)
    lax.fori_loop(4, 5, one_head, 0)

    def pass_on(hh, carry):
        got(at.at[feats(1 - zl, hh), mine], azr.at[hh])
        pass_copy(hh).start()
        return carry
    lax.fori_loop(0, LOCAL_HEADS, pass_on, 0)

    def attended_wait(hh, carry):
        got(at.at[feats(zl, hh), theirs], aor.at[hh])
        got(at.at[feats(1 - zl, hh), theirs], afr.at[hh])
        return carry
    lax.fori_loop(0, LOCAL_HEADS, attended_wait, 0)

    own = 1 - (c - row_core) * (c - row_core)

    def group_of(i):
        pair = own * (i % 4) + (1 - own) * (i // 2)
        first = own * (1 - i // 4) + (1 - own) * (1 - i % 2)
        row = own * (first * y + (1 - first) * direct_row) + (1 - own) * (
            first * direct_row + (1 - first) * ((y + 2) % NY))
        is1 = (pair % 2) * (1 - pair // 2)
        is2 = (1 - pair % 2) * (pair // 2)
        is3 = (pair % 2) * (pair // 2)
        gz = (zh + 4 - sgn * is1 + sgn * is2 + 2 * is3) % 4
        return (row % 2) * 4 + gz

    def far_wait_pair(p):
        @pl.when(jnp.logical_not(is_row_core))
        def _():
            for j in (2 * p, 2 * p + 1):
                for half in range(2):
                    got(piece((y + 2) % NY, z_of(j), half), yrr.at[half, j])

    def lane_block(xx):
        return pl.ds(al(xx * 128, 128), 128)

    def far_copies(i):
        yield rc(far_out.at[i, pl.ds(0, WC), :], far_in.at[i, 0], ffs.at[i, 0], ffr.at[i, 0],
                 dev(xp, y, z, c))
        yield rc(far_out.at[i, pl.ds(WC, WC), :], far_in.at[i, 1], ffs.at[i, 1], ffr.at[i, 1],
                 dev(xm, y, z, c))

    def near_copies(i):
        yield rc(near_out.at[i, 0], near_in.at[i, 0], nns.at[i, 0], nnr.at[i, 0], dev(xp, y, z, c))
        yield rc(near_out.at[i, 1], near_in.at[i, 1], nns.at[i, 1], nnr.at[i, 1], dev(xm, y, z, c))

    def stage_a(i):
        slot_i = i % 3
        rows = pl.ds(al(group_of(i) * GC, 32), GC)
        pf[slot_i] = jnp.dot(wt[rows, :], at[...], preferred_element_type=F32)
        far_out[i] = pf[slot_i, :, lane_block((x + 2) % NX)].astype(BF)
        for cp in far_copies(i):
            cp.start()

    def stage_b(i):
        slot_i = i % 3
        for d in range(2):
            got(far_in.at[i, d], ffr.at[i, d])
        up = lane_block(xp)
        down = lane_block(xm)
        lo, hi = pl.ds(0, WC), pl.ds(WC, WC)
        near_out[i, 0, lo, :] = (pf[slot_i, lo, up] + far_in[i, 0].astype(F32)).astype(BF)
        near_out[i, 0, hi, :] = pf[slot_i, hi, up].astype(BF)
        near_out[i, 1, lo, :] = pf[slot_i, lo, down].astype(BF)
        near_out[i, 1, hi, :] = (pf[slot_i, hi, down] + far_in[i, 1].astype(F32)).astype(BF)
        for cp in near_copies(i):
            cp.start()

    def stage_c(i):
        slot_i = i % 3
        for d in range(2):
            got(near_in.at[i, d], nnr.at[i, d])
        rows = pl.ds(al(group_of(i) * GC, 32), GC)
        ft[rows, :] = (pf[slot_i, :, lane_block(x)] + near_in[i, 0].astype(F32)
                       + near_in[i, 1].astype(F32))

    def step(i, carry):
        @pl.when(i == 2)
        def _():
            y_service(4)

        @pl.when(i == 4)
        def _():
            y_service(5)

        @pl.when(i == 5)
        def _():
            y_service(6)

        @pl.when(i == 6)
        def _():
            y_service(7)
        for p in range(4):
            @pl.when(i == 2 * p + 1)
            def _(p=p):
                far_wait_pair(p)

        @pl.when(i < GROUPS)
        def _():
            stage_a(i)

        @pl.when(jnp.logical_and(i >= 1, i < GROUPS + 1))
        def _():
            stage_b(i - 1)

        @pl.when(i >= 2)
        def _():
            stage_c(i - 2)
        return carry
    lax.fori_loop(0, GROUPS + 2, step, 0)

    def finish(b, carry):
        here = pl.ds(al(b * 128, 128), 128)
        ob[:, here] = (ft[here, :].T * gate_row[:, here]).astype(BF)
        return carry
    lax.fori_loop(0, 20, finish, 0)
    half_cols = pl.ds(al(c * 2560, 128), 2560)
    keep = pltpu.make_async_copy(
        ob.at[pl.ds(al(c * TOK, TOK), TOK), :], out_hbm.at[0, :, half_cols], finl)
    keep.start()
    give = rc(ob.at[pl.ds(al(oc * TOK, TOK), TOK), :], out_hbm.at[0, :, half_cols], fins, finr,
              other)
    give.start()

    kv_send_wait(v_hbm.at[0], vb, vs, vr)
    kv_send_wait(k_nrm, kb, ks, kr)

    def q_sent(t, carry):
        q_copy((head + t) % 8).wait_send()
        return carry
    lax.fori_loop(1, 8, q_sent, 0)

    @pl.when(jnp.logical_not(q_stays))
    def _():
        q_copy(head).wait_send()
    for buf, index in ((vb, 0), (kb, 1)):
        half = buf.at[pl.ds(al(c * 512, 512), 512), :]
        rc(half, half, fs.at[index], fr.at[index], other).wait_send()

    @pl.when(jnp.logical_not(is_row_core))
    def _():
        rc(w_own, piece(y, z, c), w0s, w0r.at[c], other).wait_send()

    @pl.when(is_row_core)
    def _():
        for d in range(2):
            for k in range(1, 5):
                z_send(d, k).wait_send()
        for cp in row_sends(z, 0):
            cp.wait_send()
        for k in range(1, 4):
            for d in range(2):
                for cp in row_sends(z_from(d, k), z_index(d, k)):
                    cp.wait_send()
        for cp in row_sends((z + 4) % NZ, 7):
            cp.wait_send()
    for j in range(8):
        relay(j).wait_send()

    def heads_sent(hh, carry):
        away_copy(hh).wait_send()
        home_copy(hh).wait_send()
        pass_copy(hh).wait_send()
        return carry
    lax.fori_loop(0, LOCAL_HEADS, heads_sent, 0)

    def sums_sent(i, carry):
        for cp in far_copies(i):
            cp.wait_send()
        for cp in near_copies(i):
            cp.wait_send()
        return carry
    lax.fori_loop(0, GROUPS, sums_sent, 0)
    keep.wait()
    give.wait_send()
    got(out_hbm.at[0, :, pl.ds(al(oc * 2560, 128), 2560)], finr)


def body(query_rows, key_rows, value_rows, query_gain, key_gain, out_weight, gate_table, lengths,
         step_index):
    vmem = pl.BlockSpec(memory_space=pltpu.VMEM)
    smem = pl.BlockSpec(memory_space=pltpu.SMEM)
    hbm = pl.BlockSpec(memory_space=pl.ANY)
    sem = pltpu.SemaphoreType.DMA
    flops = 2 * (2 * 5 * 512 * 1024 * 128 + 512 * 1280 * 2560)
    return pl.pallas_call(
        kernel,
        out_shape=jax.ShapeDtypeStruct((1, TOK, D), BF),
        in_specs=[smem, smem, hbm, hbm, hbm, vmem, vmem, hbm, hbm],
        out_specs=hbm,
        scratch_shapes=[
            pltpu.VMEM((TOK, D), BF),
            pltpu.VMEM((TOK, D), BF),
            pltpu.VMEM((TOK, D), BF),
            pltpu.VMEM((TOK, D), BF),
            pltpu.VMEM((GW, WC), BF),
            pltpu.VMEM((WC, GW), BF),
            pltpu.VMEM((STEPS, 2560), F32),
            pltpu.VMEM((1, 2560), F32),
            pltpu.VMEM((512, GW), BF),
            pltpu.VMEM((KEYS, GW), BF),
            pltpu.VMEM((KEYS, GW), BF),
            pltpu.VMEM((KEYS, 128), F32),
            pltpu.VMEM((2560, 2 * GW), BF),
            pltpu.VMEM((LOCAL_HEADS, HD, 256), BF),
            pltpu.VMEM((2 * GW, 512), BF),
            pltpu.VMEM((3, GC, 512), F32),
            pltpu.VMEM((GROUPS, GC, 128), BF),
            pltpu.VMEM((GROUPS, 2, WC, 128), BF),
            pltpu.VMEM((GROUPS, 2, GC, 128), BF),
            pltpu.VMEM((GROUPS, 2, GC, 128), BF),
            pltpu.VMEM((2560, 128), F32),
            pltpu.VMEM((128, 2560), BF),
            sem((4,)),
            sem((8,)), sem((8,)), sem((8,)), sem((8,)), sem((8,)), sem((8,)),
            sem((2,)), sem((2,)),
            sem, sem((2,)),
            sem((2, 4)), sem((2, 4)),
            sem((2, 8)), sem((8,)),
            sem((8,)), sem((2, 8)),
            sem((5,)), sem((5,)), sem((5,)), sem((5,)), sem((5,)), sem((5,)),
            sem((8, 2)), sem((8, 2)), sem((8, 2)), sem((8, 2)),
            sem, sem, sem,
        ],
        compiler_params=pltpu.CompilerParams(
            collective_id=0, has_side_effects=True, vmem_limit_bytes=48 * 2**20),
        cost_estimate=pl.CostEstimate(flops=flops, bytes_accessed=4 * 2**20,
                                      transcendentals=5 * 512 * 1024),
        name="gated_attention",
    )(lengths, step_index, query_rows, key_rows, value_rows, query_gain[None], key_gain[None],
      out_weight, gate_table)


def solution(mesh):
    placed = (
        P("slot", ("head", "blk"), None),
        P("slot", ("head", "blk"), None),
        P("slot", ("head", "blk"), None),
        P(),
        P(),
        P("head", ("slot", "blk")),
        P(),
        P("slot"),
        P("slot"),
    )
    return jax.shard_map(
        body,
        mesh=mesh,
        in_specs=placed,
        out_specs=P("slot", ("head", "blk"), None),
        check_vma=False,
    )
```

```python
import functools
import math

import jax
import jax.numpy as jnp
from jax import lax
from jax.experimental import pallas as pl
from jax.experimental.pallas import tpu as pltpu
from jax.sharding import PartitionSpec as P

HD = 128
NEG_BIG = -1e30
EPSILON = 1e-06
MESH = pl.DeviceIdType.MESH

NX, NY, NZ, NC = 4, 4, 8, 2
TOK = 64
D = 5120
GW = 640
LOCAL_HEADS = GW // HD
KEYS = 1024
WC = 160
GC = 2 * WC
GROUPS = 8
AHEAD = 2
W_STEPS = ((1, 0), (2, 1), (3, 3), (4, 5))
NEAR_LAG = 2
LAST_LAG = 4
STEPS = 50
BF = jnp.bfloat16
F32 = jnp.float32


def al(value, unit):
    return pl.multiple_of(value, unit)


def kernel(
    len_ref, step_ref, q_hbm, k_hbm, v_hbm, qg_hbm, kg_hbm, w_hbm, gt_hbm, out_hbm,
    qg_ref, kg_ref, q_raw, k_raw, v_raw, q_nrm, kv_nrm, w_own, gate_tab,
    gate_row, qb, kvb, bias, wt,
    a_stage, at, pf, far_out, far_in, near_out, near_in, ft, gate_col, pair_out, pair_in, ob,
    ld, gs, gr, qs, qr, qos, ks, kr, fs, fr, w0s, w0r, zs, zr, yds, ydr,
    azs, azr, aos, aor, afs, afr, pos, por, pas, par, pfs, pfr, ffs, ffr, nns, nnr, pss, psr, fins, finr, fink,
):
    slot = lax.axis_index("slot")
    head = lax.axis_index("head")
    c = lax.axis_index("blk")
    x, zl = head // 2, head % 2
    y, zh = slot // 4, slot % 4
    z = zh * 2 + zl
    oc = 1 - c
    row_core = y % 2
    is_row_core = c == row_core
    y_pair = y + 1 - 2 * (y % 2)
    y_row = 3 - y

    def row_of(yy):
        differs = (c - yy % 2) * (c - yy % 2)
        return (1 - differs) * yy + differs * (3 - yy)
    my_row = row_of(y)
    pair_row = row_of(y_pair)

    def dev(dx, dy, dz, dc):
        return (dy * 4 + dz // 2, dx * 2 + dz % 2, dc)

    def rc(src, dst, send, recv, device):
        return pltpu.make_async_remote_copy(
            src_ref=src, dst_ref=dst, send_sem=send, recv_sem=recv,
            device_id=device, device_id_type=MESH,
        )

    def got(ref, sem):
        pltpu.make_async_copy(ref, ref, sem).wait()

    xp, xm = (x + 1) % NX, (x + 3) % NX
    zp, zm = (z + 1) % NZ, (z + 7) % NZ
    z_mate = zh * 2 + (1 - zl)
    z_out = (z + NZ - 1 + 2 * zl) % NZ
    other = dev(x, y, z, oc)
    pair = dev(x, y_pair, z, c)

    load_w = pltpu.make_async_copy(w_hbm, w_own, ld.at[0])
    load_k = pltpu.make_async_copy(k_hbm.at[0], k_raw, ld.at[1])
    load_q = pltpu.make_async_copy(q_hbm.at[0], q_raw, ld.at[2])
    load_g = [
        pltpu.make_async_copy(
            gt_hbm.at[:, pl.ds(al(row * 1280, 128), 1280)], gate_tab.at[i], ld.at[3 + i])
        for i, row in enumerate((my_row, pair_row))
    ]
    load_kg = pltpu.make_async_copy(kg_hbm, kg_ref, ld.at[5])
    load_qg = pltpu.make_async_copy(qg_hbm, qg_ref, ld.at[6])
    load_v = pltpu.make_async_copy(v_hbm.at[0], v_raw, ld.at[7])
    load_w.start()
    load_v.start()
    load_k.start()
    load_kg.start()
    load_qg.start()
    load_q.start()
    for cp in load_g:
        cp.start()

    barrier = pltpu.get_barrier_semaphore()
    partners = []
    for dh in range(8):
        for dc in range(2):
            if (dh, dc) != (0, 0):
                ph = (head + dh) % 8
                partners.append((slot, ph, (c + dc) % 2))
    partners.append(dev(x, y, z_out, c))
    partners.append(dev(x, y_row, z, c))
    partners.append(pair)
    partners.append(dev(x, y_pair, z, oc))
    for partner in partners:
        pl.semaphore_signal(barrier, inc=1, device_id=partner, device_id_type=MESH)
    pl.semaphore_wait(barrier, len(partners))

    def cols(ref, group):
        return ref.at[:, pl.ds(al(group * GW, 128), GW)]

    def kv_lanes(hh):
        return pl.ds(al(hh * 2 * HD, 2 * HD), 2 * HD)

    def q_lanes(hh):
        return pl.ds(al(hh * HD, HD), HD)

    def kv_place(hh):
        return kvb.at[pl.ds(al(c * 512 + head * TOK, TOK), TOK), kv_lanes(hh)]

    def kv_part(group, hh):
        return kv_nrm.at[:, pl.ds(al(group * 2 * GW + hh * 2 * HD, 2 * HD), 2 * HD)]

    def kv_half(which_c, hh):
        return kvb.at[pl.ds(al(which_c * 512, 512), 512), kv_lanes(hh)]

    def kv_pass(hh):
        ref = kv_half(c, hh)
        return rc(ref, ref, fs.at[hh], fr.at[hh], other)

    q_core = x // 2
    q_stays = c == q_core
    q_row = zl * 256 + (x % 2) * 128 + c * TOK

    def q_place(hh):
        return qb.at[pl.ds(al(q_row, TOK), TOK), q_lanes(hh)]

    def q_part(group, hh):
        return q_nrm.at[:, pl.ds(al(group * GW + hh * HD, HD), HD)]

    def q_copy(group, hh, send):
        return rc(q_part(group, hh), q_place(hh), send, qr.at[hh], (slot, group, q_core))

    def send_head(hh):
        pltpu.make_async_copy(kv_part(head, hh), kv_place(hh), kr.at[hh]).start()

        @pl.when(q_stays)
        def _():
            pltpu.make_async_copy(q_part(head, hh), q_place(hh), qr.at[hh]).start()

        @pl.when(jnp.logical_not(q_stays))
        def _():
            q_copy(head, hh, qos.at[hh]).start()

        def one(t, carry):
            group = (head + t) % 8
            rc(kv_part(group, hh), kv_place(hh), ks.at[hh], kr.at[hh], (slot, group, c)).start()
            q_copy(group, hh, qs.at[hh]).start()
            return carry
        lax.fori_loop(1, 8, one, 0)

    def head_sent(hh):
        got(kvb.at[pl.ds(0, 7 * TOK), kv_lanes(hh)], ks.at[hh])
        got(qb.at[pl.ds(0, 7 * TOK), q_lanes(hh)], qs.at[hh])

    def head_here(hh):
        got(kv_half(c, hh), kr.at[hh])
        kv_pass(hh).start()
        got(qb.at[:, q_lanes(hh)], qr.at[hh])
        got(kv_half(oc, hh), fr.at[hh])

    def piece(zsrc, half=None):
        row = (zsrc // 2) * GC
        size = GC
        if half is not None:
            row = row + half * WC
            size = WC
        return wt.at[pl.ds(al(row, 32), size), pl.ds(al((zsrc % 2) * GW, 128), GW)]

    load_w.wait()

    @pl.when(is_row_core)
    def _():
        pltpu.make_async_copy(w_own, piece(z, c), w0r.at[c]).start()

    @pl.when(jnp.logical_not(is_row_core))
    def _():
        rc(w_own, piece(z, c), w0s, w0r.at[c], other).start()

    def row_send(zsrc, j):
        return rc(piece(zsrc), piece(zsrc), yds.at[j], ydr.at[j], dev(x, y_row, z, c))

    def z_send(d, k):
        zsrc = (z + NZ - (k - 1)) % NZ if d == 0 else (z + k - 1) % NZ
        half = None if k < 4 else d
        return rc(piece(zsrc, half), piece(zsrc, half), zs.at[d, k - 1], zr.at[d, k - 1],
                  dev(x, y, zp if d == 0 else zm, c))

    def z_from(d, k):
        return (z + NZ - k) % NZ if d == 0 else (z + k) % NZ

    def z_index(d, k):
        ahead = zl if d == 0 else 1 - zl
        if k == 1:
            return 2 - ahead
        if k == 2:
            return 3 + ahead
        return 6 - ahead

    def z_first():
        @pl.when(is_row_core)
        def _():
            got(piece(z, 0), w0r.at[0])
            got(piece(z, 1), w0r.at[1])
            for d in range(2):
                z_send(d, 1).start()
            row_send(z, 0).start()

    def z_service(k):
        @pl.when(is_row_core)
        def _():
            for d in range(2):
                zsrc = z_from(d, k)
                got(piece(zsrc), zr.at[d, k - 1])
                z_send(d, k + 1).start()
                row_send(zsrc, z_index(d, k)).start()

    def z_last():
        @pl.when(is_row_core)
        def _():
            zsrc = (z + 4) % NZ
            for d in range(2):
                got(piece(zsrc, d), zr.at[d, 3])
            row_send(zsrc, 7).start()

    sgn = 1 - 2 * zl
    DELTA = (0, 1, -1, -2, 2, 3, -3, 4)

    def z_of(j):
        return (z + NZ + sgn * DELTA[j]) % NZ

    def row_wait(p):
        @pl.when(jnp.logical_not(is_row_core))
        def _():
            for j in (2 * p, 2 * p + 1):
                got(piece(z_of(j)), ydr.at[j])

    def normed(raw, gain_ref, here):
        vals = raw[here, :].astype(F32)
        mean_square = jnp.mean(vals * vals, axis=-1, keepdims=True)
        return (vals * lax.rsqrt(mean_square + EPSILON) * gain_ref[...]).astype(BF)

    def kv_rows(i, carry):
        here = pl.ds(al(i * 16, 16), 16)
        out = normed(k_raw, kg_ref, here)
        for hh in range(D // HD):
            src = slice(hh * HD, hh * HD + HD)
            kv_nrm[here, hh * 2 * HD:hh * 2 * HD + HD] = out[:, src]
            kv_nrm[here, hh * 2 * HD + HD:hh * 2 * HD + 2 * HD] = v_raw[here, src]
        return carry

    def q_rows(i, carry):
        here = pl.ds(al(i * 16, 16), 16)
        q_nrm[here, :] = normed(q_raw, qg_ref, here)
        return carry

    load_k.wait()
    load_kg.wait()
    load_v.wait()
    lax.fori_loop(0, TOK // 16, kv_rows, 0)
    load_q.wait()
    load_qg.wait()
    lax.fori_loop(0, TOK // 16, q_rows, 0)
    send_head(0)
    z_first()
    for hh in range(1, AHEAD):
        send_head(hh)

    def mask_rows(i, carry):
        row = lax.broadcasted_iota(jnp.int32, (TOK, 128), 0)
        pos = (i % 8) * 128 + (i // 8) * TOK + row
        bias[pl.ds(al(i * TOK, TOK), TOK), :] = jnp.where(pos < len_ref[0], 0.0, NEG_BIG)
        return carry
    lax.fori_loop(0, KEYS // TOK, mask_rows, 0)

    step_rows = lax.broadcasted_iota(jnp.int32, (STEPS, 1280), 0)
    for i in range(2):
        load_g[i].wait()
        gate_row[i] = jnp.sum(
            jnp.where(step_rows == step_ref[0], gate_tab[i], 0.0), axis=0, keepdims=True)
    gate_copy = rc(gate_row.at[1], gate_row.at[2], gs, gr, pair)
    gate_copy.start()

    scale = math.log2(math.e) / math.sqrt(HD)
    mine = pl.ds(al(c * 256, 128), 256)
    theirs = pl.ds(al(oc * 256, 128), 256)
    pair_mine = pl.ds(al(512 + c * 256, 128), 256)
    pair_theirs = pl.ds(al(512 + oc * 256, 128), 256)

    def feats(which_zl, hh):
        return pl.ds(al(which_zl * GW + hh * HD, HD), HD)

    def attend(hh, zq):
        lanes = q_lanes(hh)
        keys = kvb[:, pl.ds(al(hh * 2 * HD, HD), HD)]
        values = kvb[:, pl.ds(al(hh * 2 * HD + HD, HD), HD)]
        queries = qb[pl.ds(al(zq * 256, 256), 256), lanes]
        scores = lax.dot_general(keys, queries, (((1,), (1,)), ((), ())),
                                 preferred_element_type=F32)
        scores = scores * scale + jnp.concatenate([bias[...], bias[...]], axis=1)
        top = jnp.max(scores, axis=0, keepdims=True)
        weights = jnp.exp2(scores - top)
        total = jnp.sum(weights, axis=0, keepdims=True)
        mixed = lax.dot_general(values, weights.astype(BF), (((0,), (0,)), ((), ())),
                                preferred_element_type=F32)
        return (mixed / total).astype(BF)

    def away_copy(hh):
        return rc(a_stage.at[hh], at.at[feats(zl, hh), mine], azs.at[hh], azr.at[hh],
                  dev(x, y, z_mate, c))

    def home_copy(hh):
        ref = at.at[feats(zl, hh), mine]
        return rc(ref, ref, aos.at[hh], aor.at[hh], other)

    def pass_copy(hh):
        ref = at.at[feats(1 - zl, hh), mine]
        return rc(ref, ref, afs.at[hh], afr.at[hh], other)

    def pair_home_copy(hh):
        return rc(at.at[feats(zl, hh), mine], at.at[feats(zl, hh), pair_mine],
                  pos.at[hh], por.at[hh], pair)

    def pair_pass_copy(hh):
        return rc(at.at[feats(1 - zl, hh), mine], at.at[feats(1 - zl, hh), pair_mine],
                  pas.at[hh], par.at[hh], pair)

    def pair_share_copy(hh, which):
        ref = at.at[feats(which, hh), pair_mine]
        return rc(ref, ref, pfs.at[hh, which], pfr.at[hh, which], other)

    def one_head(hh):
        a_stage[hh] = attend(hh, 1 - zl)
        away_copy(hh).start()
        at[feats(zl, hh), mine] = attend(hh, zl)
        pair_home_copy(hh).start()
        home_copy(hh).start()

    def pass_on(hh, carry):
        got(at.at[feats(1 - zl, hh), mine], azr.at[hh])
        pair_pass_copy(hh).start()
        pass_copy(hh).start()
        return carry

    def w_steps(hh):
        for k, when in W_STEPS:
            @pl.when(hh == when)
            def _(k=k):
                z_service(k) if k < 4 else z_last()

    def heads(hh, carry):
        w_steps(hh)

        @pl.when(hh + AHEAD < LOCAL_HEADS)
        def _():
            head_sent(hh)
            send_head(hh + AHEAD)
        head_here(hh)
        one_head(hh)

        @pl.when(hh > 0)
        def _():
            pass_on(hh - 1, 0)
        return carry
    lax.fori_loop(0, LOCAL_HEADS, heads, 0)
    w_steps(LOCAL_HEADS)
    pass_on(LOCAL_HEADS - 1, 0)

    def attended_wait(hh, carry):
        got(at.at[feats(zl, hh), theirs], aor.at[hh])
        got(at.at[feats(1 - zl, hh), theirs], afr.at[hh])
        return carry
    lax.fori_loop(0, LOCAL_HEADS, attended_wait, 0)

    def pair_share(hh, carry):
        got(at.at[feats(zl, hh), pair_mine], por.at[hh])
        pair_share_copy(hh, zl).start()
        got(at.at[feats(1 - zl, hh), pair_mine], par.at[hh])
        pair_share_copy(hh, 1 - zl).start()
        return carry

    def pair_wait(hh, carry):
        for which in range(2):
            got(at.at[feats(which, hh), pair_theirs], pfr.at[hh, which])
        return carry

    def past(i, k):
        return jnp.where(i >= k, 1, 0)

    def slot_of(i):
        return past(i, 2) - past(i, 4) + past(i, 5) - past(i, 7)

    def group_p(i):
        return past(i, 1) - past(i, 2) + past(i, 3) + past(i, 4) + past(i, 6)

    def group_of(i):
        return zh_of(group_p(i))

    def zh_of(p):
        is1 = (p % 2) * (1 - p // 2)
        is2 = (1 - p % 2) * (p // 2)
        is3 = (p % 2) * (p // 2)
        return (zh + 4 - sgn * is1 + sgn * is2 + 2 * is3) % 4

    def lane_block(xx):
        return pl.ds(al(xx * 128, 128), 128)

    def far_copies(i):
        yield rc(far_out.at[i, pl.ds(0, WC), :], far_in.at[i, 0], ffs.at[i, 0], ffr.at[i, 0],
                 dev(xp, y, z, c))
        yield rc(far_out.at[i, pl.ds(WC, WC), :], far_in.at[i, 1], ffs.at[i, 1], ffr.at[i, 1],
                 dev(xm, y, z, c))

    def near_copies(i):
        yield rc(near_out.at[i, 0], near_in.at[i, 0], nns.at[i, 0], nnr.at[i, 0], dev(xp, y, z, c))
        yield rc(near_out.at[i, 1], near_in.at[i, 1], nns.at[i, 1], nnr.at[i, 1], dev(xm, y, z, c))

    def stage_a(i):
        rows = pl.ds(al(group_of(i) * GC, 32), GC)
        lanes = pl.ds(al(slot_of(i) * 512, 128), 512)
        pf[i] = jnp.dot(wt[rows, :], at[:, lanes], preferred_element_type=F32)
        far_out[i] = pf[i, :, lane_block((x + 2) % NX)].astype(BF)
        for cp in far_copies(i):
            cp.start()

    def stage_b(i):
        for d in range(2):
            got(far_in.at[i, d], ffr.at[i, d])
        up = lane_block(xp)
        down = lane_block(xm)
        lo, hi = pl.ds(0, WC), pl.ds(WC, WC)
        near_out[i, 0, lo, :] = (pf[i, lo, up] + far_in[i, 0].astype(F32)).astype(BF)
        near_out[i, 0, hi, :] = pf[i, hi, up].astype(BF)
        near_out[i, 1, lo, :] = pf[i, lo, down].astype(BF)
        near_out[i, 1, hi, :] = (pf[i, hi, down] + far_in[i, 1].astype(F32)).astype(BF)
        for cp in near_copies(i):
            cp.start()

    def stage_c(i):
        for d in range(2):
            got(near_in.at[i, d], nnr.at[i, d])
        rows = pl.ds(al(group_of(i) * GC, 32), GC)
        total = (pf[i, :, lane_block(x)] + near_in[i, 0].astype(F32)
                 + near_in[i, 1].astype(F32))
        whose = slot_of(i)

        @pl.when(whose == 0)
        def _():
            ft[rows, :] = total

        @pl.when(whose == 1)
        def _():
            pair_out[rows, :] = (total * gate_col[rows, :]).astype(BF)
            pair_sum(group_p(i)).start()

    def pair_sum(p):
        rows = pl.ds(al(zh_of(p) * GC, 32), GC)
        return rc(pair_out.at[rows, :], pair_in.at[rows, :], pss.at[p], psr.at[p], pair)

    def step(i, carry):
        for p, when in enumerate((0, 1, 4, 6)):
            @pl.when(i == when)
            def _(p=p):
                row_wait(p)

        @pl.when(i == 1)
        def _():
            lax.fori_loop(0, LOCAL_HEADS, pair_share, 0)

        @pl.when(i == 2)
        def _():
            lax.fori_loop(0, LOCAL_HEADS, pair_wait, 0)

        @pl.when(i < GROUPS)
        def _():
            stage_a(i)

        @pl.when(jnp.logical_and(i >= NEAR_LAG, i < GROUPS + NEAR_LAG))
        def _():
            stage_b(i - NEAR_LAG)

        @pl.when(i >= LAST_LAG)
        def _():
            stage_c(i - LAST_LAG)
        return carry
    def tokens(which, cc):
        return ob.at[which, pl.ds(al(cc * TOK, TOK), TOK), :]

    def out_cols(row):
        return out_hbm.at[0, :, pl.ds(al(row * 1280, 128), 1280)]

    keep = [pltpu.make_async_copy(tokens(i, c), out_cols(row), fink.at[i])
            for i, row in enumerate((my_row, pair_row))]
    give = [rc(tokens(i, oc), out_cols(row), fins.at[i], finr.at[i], other)
            for i, row in enumerate((my_row, pair_row))]
    got(gate_row.at[2], gr)
    gate_col[...] = jnp.broadcast_to(gate_row[2], (128, 1280)).T
    lax.fori_loop(0, GROUPS + LAST_LAG - 1, step, 0)
    stage_c(GROUPS - 1)
    for b in range(10):
        here = slice(b * 128, b * 128 + 128)
        ob[0, :, here] = (ft[here, :].T * gate_row[0, :, here]).astype(BF)
    keep[0].start()
    give[0].start()
    for p in range(4):
        got(pair_in.at[pl.ds(al(zh_of(p) * GC, 32), GC), :], psr.at[p])
    for b in range(10):
        here = slice(b * 128, b * 128 + 128)
        ob[1, :, here] = pair_in[here, :].T
    keep[1].start()
    give[1].start()

    for hh in range(LOCAL_HEADS - AHEAD, LOCAL_HEADS):
        head_sent(hh)

    def head_passed(hh, carry):
        @pl.when(jnp.logical_not(q_stays))
        def _():
            q_copy(head, hh, qos.at[hh]).wait_send()
        kv_pass(hh).wait_send()
        return carry
    lax.fori_loop(0, LOCAL_HEADS, head_passed, 0)

    @pl.when(jnp.logical_not(is_row_core))
    def _():
        rc(w_own, piece(z, c), w0s, w0r.at[c], other).wait_send()

    @pl.when(is_row_core)
    def _():
        for d in range(2):
            for k in range(1, 5):
                z_send(d, k).wait_send()
        row_send(z, 0).wait_send()
        for k in range(1, 4):
            for d in range(2):
                row_send(z_from(d, k), z_index(d, k)).wait_send()
        row_send((z + 4) % NZ, 7).wait_send()

    def heads_sent(hh, carry):
        away_copy(hh).wait_send()
        home_copy(hh).wait_send()
        pass_copy(hh).wait_send()
        pair_home_copy(hh).wait_send()
        pair_pass_copy(hh).wait_send()
        for which in range(2):
            pair_share_copy(hh, which).wait_send()
        return carry
    lax.fori_loop(0, LOCAL_HEADS, heads_sent, 0)

    def sums_sent(i, carry):
        for cp in far_copies(i):
            cp.wait_send()
        for cp in near_copies(i):
            cp.wait_send()
        return carry
    lax.fori_loop(0, GROUPS, sums_sent, 0)
    gate_copy.wait_send()
    for p in range(4):
        pair_sum(p).wait_send()
    for i, yy in enumerate((y, y_pair)):
        keep[i].wait()
        give[i].wait_send()
        differs = (oc - yy % 2) * (oc - yy % 2)
        got(out_cols((1 - differs) * yy + differs * (3 - yy)), finr.at[i])


def body(query_rows, key_rows, value_rows, query_gain, key_gain, out_weight, gate_table, lengths,
         step_index):
    smem = pl.BlockSpec(memory_space=pltpu.SMEM)
    hbm = pl.BlockSpec(memory_space=pl.ANY)
    sem = pltpu.SemaphoreType.DMA
    flops = 2 * (2 * 5 * 512 * 1024 * 128 + 512 * 1280 * 2560)
    return pl.pallas_call(
        kernel,
        out_shape=jax.ShapeDtypeStruct((1, TOK, D), BF),
        in_specs=[smem, smem] + [hbm] * 7,
        out_specs=hbm,
        scratch_shapes=[
            pltpu.VMEM((1, D), F32),
            pltpu.VMEM((1, D), F32),
            pltpu.VMEM((TOK, D), BF),
            pltpu.VMEM((TOK, D), BF),
            pltpu.VMEM((TOK, D), BF),
            pltpu.VMEM((TOK, D), BF),
            pltpu.VMEM((TOK, 2 * D), BF),
            pltpu.VMEM((WC, GW), BF),
            pltpu.VMEM((2, STEPS, 1280), F32),
            pltpu.VMEM((3, 1, 1280), F32),
            pltpu.VMEM((512, GW), BF),
            pltpu.VMEM((KEYS, 2 * GW), BF),
            pltpu.VMEM((KEYS, 128), F32),
            pltpu.VMEM((1280, 2 * GW), BF),
            pltpu.VMEM((LOCAL_HEADS, HD, 256), BF),
            pltpu.VMEM((2 * GW, 1024), BF),
            pltpu.VMEM((GROUPS, GC, 512), F32),
            pltpu.VMEM((GROUPS, GC, 128), BF),
            pltpu.VMEM((GROUPS, 2, WC, 128), BF),
            pltpu.VMEM((GROUPS, 2, GC, 128), BF),
            pltpu.VMEM((GROUPS, 2, GC, 128), BF),
            pltpu.VMEM((1280, 128), F32),
            pltpu.VMEM((1280, 128), F32),
            pltpu.VMEM((1280, 128), BF),
            pltpu.VMEM((1280, 128), BF),
            pltpu.VMEM((2, 128, 1280), BF),
            sem((8,)),
            sem, sem,
            sem((5,)), sem((5,)), sem((5,)), sem((5,)), sem((5,)),
            sem((5,)), sem((5,)),
            sem, sem((2,)),
            sem((2, 4)), sem((2, 4)),
            sem((8,)), sem((8,)),
            sem((5,)), sem((5,)), sem((5,)), sem((5,)), sem((5,)), sem((5,)),
            sem((5,)), sem((5,)), sem((5,)), sem((5,)), sem((5, 2)), sem((5, 2)),
            sem((8, 2)), sem((8, 2)), sem((8, 2)), sem((8, 2)),
            sem((4,)), sem((4,)),
            sem((2,)), sem((2,)), sem((2,)),
        ],
        compiler_params=pltpu.CompilerParams(
            collective_id=0, has_side_effects=True, vmem_limit_bytes=60 * 2**20),
        cost_estimate=pl.CostEstimate(flops=flops, bytes_accessed=4 * 2**20,
                                      transcendentals=5 * 512 * 1024),
        name="gated_attention",
    )(lengths, step_index, query_rows, key_rows, value_rows, query_gain[None], key_gain[None],
      out_weight.T, gate_table)


def solution(mesh):
    placed = (
        P("slot", ("head", "blk"), None),
        P("slot", ("head", "blk"), None),
        P("slot", ("head", "blk"), None),
        P(),
        P(),
        P("head", ("slot", "blk")),
        P(),
        P("slot"),
        P("slot"),
    )
    return jax.shard_map(
        body,
        mesh=mesh,
        in_specs=placed,
        out_specs=P("slot", ("head", "blk"), None),
        check_vma=False,
    )
```

```python
import functools
import math

import jax
import jax.numpy as jnp
from jax import lax
from jax.experimental import pallas as pl
from jax.experimental.pallas import tpu as pltpu
from jax.sharding import PartitionSpec as P

HD = 128
NEG_BIG = -1e30
EPSILON = 1e-06
MESH = pl.DeviceIdType.MESH

NX, NY, NZ, NC = 4, 4, 8, 2
TOK = 64
D = 5120
GW = 640
LOCAL_HEADS = GW // HD
KEYS = 1024
WC = 160
GC = 2 * WC
GROUPS = 8
AHEAD = 2
W_STEPS = ((-1, 1), (1, 1), (-2, 3), (2, 3), (-3, 5), (3, 5), (-4, 12))
NEAR_LAG = 2
LAST_LAG = 4
STEPS = 50
BF = jnp.bfloat16
F32 = jnp.float32


def al(value, unit):
    return pl.multiple_of(value, unit)


def kernel(
    len_ref, step_ref, q_hbm, k_hbm, v_hbm, qg_hbm, kg_hbm, w_hbm, gt_hbm, out_hbm,
    qg_ref, kg_ref, q_raw, k_raw, v_raw, q_nrm, kv_nrm, w_own, gate_tab,
    gate_row, qb, kvb, bias, wt,
    a_stage, at, pf, far_out, far_in, near_out, near_in, ft, gate_col, pair_out, pair_in, ob,
    ld, gs, gr, qs, qr, qos, ks, kr, fs, fr, w0s, w0r, zs, zr, yds, ydr,
    azs, azr, aos, aor, afs, afr, pos, por, pas, par, pfs, pfr, ffs, ffr, nns, nnr, pss, psr, fins, finr, fink,
):
    slot = lax.axis_index("slot")
    head = lax.axis_index("head")
    c = lax.axis_index("blk")
    x, zl = head // 2, head % 2
    y, zh = slot // 4, slot % 4
    z = zh * 2 + zl
    oc = 1 - c
    row_core = y % 2
    is_row_core = c == row_core
    y_pair = y + 1 - 2 * (y % 2)
    y_row = 3 - y

    def row_of(yy):
        differs = (c - yy % 2) * (c - yy % 2)
        return (1 - differs) * yy + differs * (3 - yy)
    my_row = row_of(y)
    pair_row = row_of(y_pair)

    def dev(dx, dy, dz, dc):
        return (dy * 4 + dz // 2, dx * 2 + dz % 2, dc)

    def rc(src, dst, send, recv, device):
        return pltpu.make_async_remote_copy(
            src_ref=src, dst_ref=dst, send_sem=send, recv_sem=recv,
            device_id=device, device_id_type=MESH,
        )

    def got(ref, sem):
        pltpu.make_async_copy(ref, ref, sem).wait()

    xp, xm = (x + 1) % NX, (x + 3) % NX
    zp, zm = (z + 1) % NZ, (z + 7) % NZ
    z_mate = zh * 2 + (1 - zl)
    z_out = (z + NZ - 1 + 2 * zl) % NZ
    other = dev(x, y, z, oc)
    pair = dev(x, y_pair, z, c)

    load_w = pltpu.make_async_copy(w_hbm, w_own, ld.at[0])
    load_k = pltpu.make_async_copy(k_hbm.at[0], k_raw, ld.at[1])
    load_q = pltpu.make_async_copy(q_hbm.at[0], q_raw, ld.at[2])
    load_g = [
        pltpu.make_async_copy(
            gt_hbm.at[:, pl.ds(al(row * 1280, 128), 1280)], gate_tab.at[i], ld.at[3 + i])
        for i, row in enumerate((my_row, pair_row))
    ]
    load_kg = pltpu.make_async_copy(kg_hbm, kg_ref, ld.at[5])
    load_qg = pltpu.make_async_copy(qg_hbm, qg_ref, ld.at[6])
    load_v = pltpu.make_async_copy(v_hbm.at[0], v_raw, ld.at[7])
    load_w.start()
    load_v.start()
    load_k.start()
    load_kg.start()
    load_qg.start()
    load_q.start()
    for cp in load_g:
        cp.start()

    barrier = pltpu.get_barrier_semaphore()
    partners = []
    for dh in range(8):
        for dc in range(2):
            if (dh, dc) != (0, 0):
                ph = (head + dh) % 8
                partners.append((slot, ph, (c + dc) % 2))
    partners.append(dev(x, y, z_out, c))
    partners.append(dev(x, y_row, z, c))
    partners.append(pair)
    partners.append(dev(x, y_pair, z, oc))
    for partner in partners:
        pl.semaphore_signal(barrier, inc=1, device_id=partner, device_id_type=MESH)
    pl.semaphore_wait(barrier, len(partners))

    def cols(ref, group):
        return ref.at[:, pl.ds(al(group * GW, 128), GW)]

    def kv_lanes(hh):
        return pl.ds(al(hh * 2 * HD, 2 * HD), 2 * HD)

    def q_lanes(hh):
        return pl.ds(al(hh * HD, HD), HD)

    def kv_place(hh):
        return kvb.at[pl.ds(al(c * 512 + head * TOK, TOK), TOK), kv_lanes(hh)]

    def kv_part(group, hh):
        return kv_nrm.at[:, pl.ds(al(group * 2 * GW + hh * 2 * HD, 2 * HD), 2 * HD)]

    def kv_half(which_c, hh):
        return kvb.at[pl.ds(al(which_c * 512, 512), 512), kv_lanes(hh)]

    def kv_pass(hh):
        ref = kv_half(c, hh)
        return rc(ref, ref, fs.at[hh], fr.at[hh], other)

    q_core = x // 2
    q_stays = c == q_core
    q_row = zl * 256 + (x % 2) * 128 + c * TOK

    def q_place(hh):
        return qb.at[pl.ds(al(q_row, TOK), TOK), q_lanes(hh)]

    def q_part(group, hh):
        return q_nrm.at[:, pl.ds(al(group * GW + hh * HD, HD), HD)]

    def q_copy(group, hh, send):
        return rc(q_part(group, hh), q_place(hh), send, qr.at[hh], (slot, group, q_core))

    def send_head(hh):
        pltpu.make_async_copy(kv_part(head, hh), kv_place(hh), kr.at[hh]).start()

        @pl.when(q_stays)
        def _():
            pltpu.make_async_copy(q_part(head, hh), q_place(hh), qr.at[hh]).start()

        @pl.when(jnp.logical_not(q_stays))
        def _():
            q_copy(head, hh, qos.at[hh]).start()

        def one(t, carry):
            group = (head + t) % 8
            rc(kv_part(group, hh), kv_place(hh), ks.at[hh], kr.at[hh], (slot, group, c)).start()
            q_copy(group, hh, qs.at[hh]).start()
            return carry
        lax.fori_loop(1, 8, one, 0)

    def head_sent(hh):
        got(kvb.at[pl.ds(0, 7 * TOK), kv_lanes(hh)], ks.at[hh])
        got(qb.at[pl.ds(0, 7 * TOK), q_lanes(hh)], qs.at[hh])

    def head_here(hh):
        got(kv_half(c, hh), kr.at[hh])
        kv_pass(hh).start()
        got(qb.at[:, q_lanes(hh)], qr.at[hh])
        got(kv_half(oc, hh), fr.at[hh])

    def piece(zsrc, half=None):
        row = (zsrc // 2) * GC
        size = GC
        if half is not None:
            row = row + half * WC
            size = WC
        return wt.at[pl.ds(al(row, 32), size), pl.ds(al((zsrc % 2) * GW, 128), GW)]

    load_w.wait()

    @pl.when(is_row_core)
    def _():
        pltpu.make_async_copy(w_own, piece(z, c), w0r.at[c]).start()

    @pl.when(jnp.logical_not(is_row_core))
    def _():
        rc(w_own, piece(z, c), w0s, w0r.at[c], other).start()

    def row_send(zsrc, j):
        return rc(piece(zsrc), piece(zsrc), yds.at[j], ydr.at[j], dev(x, y_row, z, c))

    def z_send(d, k):
        zsrc = (z + NZ - (k - 1)) % NZ if d == 0 else (z + k - 1) % NZ
        return rc(piece(zsrc), piece(zsrc), zs.at[d, k - 1], zr.at[d, k - 1],
                  dev(x, y, zp if d == 0 else zm, c))

    def z_from(d, k):
        return (z + NZ - k) % NZ if d == 0 else (z + k) % NZ

    def z_index(d, k):
        ahead = zl if d == 0 else 1 - zl
        if k == 1:
            return 2 - ahead
        if k == 2:
            return 3 + ahead
        return 6 - ahead

    def z_first():
        @pl.when(is_row_core)
        def _():
            got(piece(z, 0), w0r.at[0])
            got(piece(z, 1), w0r.at[1])
            for d in range(2):
                z_send(d, 1).start()
            row_send(z, 0).start()

    def z_take(k):
        @pl.when(is_row_core)
        def _():
            for d in range(2):
                zsrc = z_from(d, k)
                got(piece(zsrc), zr.at[d, k - 1])
                row_send(zsrc, z_index(d, k)).start()

    def z_on(k):
        @pl.when(is_row_core)
        def _():
            for d in range(2):
                if k < 3:
                    z_send(d, k + 1).start()
                else:
                    @pl.when(d == 1 - zl)
                    def _(d=d):
                        z_send(d, 4).start()

    def z_last():
        @pl.when(is_row_core)
        def _():
            zsrc = (z + 4) % NZ
            got(piece(zsrc), zr.at[zl, 3])
            row_send(zsrc, 7).start()

    sgn = 1 - 2 * zl
    DELTA = (0, 1, -1, -2, 2, 3, -3, 4)

    def z_of(j):
        return (z + NZ + sgn * DELTA[j]) % NZ

    def row_wait(p):
        @pl.when(jnp.logical_not(is_row_core))
        def _():
            for j in (2 * p, 2 * p + 1):
                got(piece(z_of(j)), ydr.at[j])

    def normed(raw, gain_ref, here):
        vals = raw[here, :].astype(F32)
        mean_square = jnp.mean(vals * vals, axis=-1, keepdims=True)
        return (vals * lax.rsqrt(mean_square + EPSILON) * gain_ref[...]).astype(BF)

    def kv_rows(i, carry):
        here = pl.ds(al(i * 16, 16), 16)
        out = normed(k_raw, kg_ref, here)
        for hh in range(D // HD):
            src = slice(hh * HD, hh * HD + HD)
            kv_nrm[here, hh * 2 * HD:hh * 2 * HD + HD] = out[:, src]
            kv_nrm[here, hh * 2 * HD + HD:hh * 2 * HD + 2 * HD] = v_raw[here, src]
        return carry

    def q_rows(i, carry):
        here = pl.ds(al(i * 16, 16), 16)
        q_nrm[here, :] = normed(q_raw, qg_ref, here)
        return carry

    load_k.wait()
    load_kg.wait()
    load_v.wait()
    lax.fori_loop(0, TOK // 16, kv_rows, 0)
    load_q.wait()
    load_qg.wait()
    lax.fori_loop(0, TOK // 16, q_rows, 0)
    send_head(0)
    z_first()
    for hh in range(1, AHEAD):
        send_head(hh)

    def mask_rows(i, carry):
        row = lax.broadcasted_iota(jnp.int32, (TOK, 128), 0)
        pos = (i % 8) * 128 + (i // 8) * TOK + row
        bias[pl.ds(al(i * TOK, TOK), TOK), :] = jnp.where(pos < len_ref[0], 0.0, NEG_BIG)
        return carry
    lax.fori_loop(0, KEYS // TOK, mask_rows, 0)

    step_rows = lax.broadcasted_iota(jnp.int32, (STEPS, 1280), 0)
    for i in range(2):
        load_g[i].wait()
        gate_row[i] = jnp.sum(
            jnp.where(step_rows == step_ref[0], gate_tab[i], 0.0), axis=0, keepdims=True)
    gate_copy = rc(gate_row.at[1], gate_row.at[2], gs, gr, pair)
    gate_copy.start()

    got(gate_row.at[2], gr)
    gate_col[...] = jnp.broadcast_to(gate_row[2], (128, 1280)).T

    scale = math.log2(math.e) / math.sqrt(HD)
    mine = pl.ds(al(c * 256, 128), 256)
    theirs = pl.ds(al(oc * 256, 128), 256)
    pair_mine = pl.ds(al(512 + c * 256, 128), 256)
    pair_theirs = pl.ds(al(512 + oc * 256, 128), 256)

    def feats(which_zl, hh):
        return pl.ds(al(which_zl * GW + hh * HD, HD), HD)

    def attend(hh, zq):
        lanes = q_lanes(hh)
        keys = kvb[:, pl.ds(al(hh * 2 * HD, HD), HD)]
        values = kvb[:, pl.ds(al(hh * 2 * HD + HD, HD), HD)]
        queries = qb[pl.ds(al(zq * 256, 256), 256), lanes]
        scores = lax.dot_general(keys, queries, (((1,), (1,)), ((), ())),
                                 preferred_element_type=F32)
        scores = scores * scale + jnp.concatenate([bias[...], bias[...]], axis=1)
        top = jnp.max(scores, axis=0, keepdims=True)
        weights = jnp.exp2(scores - top)
        total = jnp.sum(weights, axis=0, keepdims=True)
        mixed = lax.dot_general(values, weights.astype(BF), (((0,), (0,)), ((), ())),
                                preferred_element_type=F32)
        return (mixed / total).astype(BF)

    def away_copy(hh):
        return rc(a_stage.at[hh], at.at[feats(zl, hh), mine], azs.at[hh], azr.at[hh],
                  dev(x, y, z_mate, c))

    def home_copy(hh):
        ref = at.at[feats(zl, hh), mine]
        return rc(ref, ref, aos.at[hh], aor.at[hh], other)

    def pass_copy(hh):
        ref = at.at[feats(1 - zl, hh), mine]
        return rc(ref, ref, afs.at[hh], afr.at[hh], other)

    def pair_home_copy(hh):
        return rc(at.at[feats(zl, hh), mine], at.at[feats(zl, hh), pair_mine],
                  pos.at[hh], por.at[hh], pair)

    def pair_pass_copy(hh):
        return rc(at.at[feats(1 - zl, hh), mine], at.at[feats(1 - zl, hh), pair_mine],
                  pas.at[hh], par.at[hh], pair)

    def pair_share_copy(hh, which):
        ref = at.at[feats(which, hh), pair_mine]
        return rc(ref, ref, pfs.at[hh, which], pfr.at[hh, which], other)

    def one_head(hh):
        a_stage[hh] = attend(hh, 1 - zl)
        away_copy(hh).start()
        at[feats(zl, hh), mine] = attend(hh, zl)
        pair_home_copy(hh).start()
        home_copy(hh).start()

    def pass_on(hh, carry):
        got(at.at[feats(1 - zl, hh), mine], azr.at[hh])
        pair_pass_copy(hh).start()
        pass_copy(hh).start()
        return carry

    def w_steps(hh, first=0):
        for k, when in W_STEPS:
            if first <= when < first + 10:
                @pl.when(hh == when - first)
                def _(k=k):
                    if k == -4:
                        z_last()
                    else:
                        z_take(-k) if k < 0 else z_on(k)

    def heads(hh, carry):
        w_steps(hh)

        @pl.when(hh + AHEAD < LOCAL_HEADS)
        def _():
            head_sent(hh)
            send_head(hh + AHEAD)
        head_here(hh)
        one_head(hh)

        @pl.when(hh > 0)
        def _():
            pass_on(hh - 1, 0)
        return carry
    lax.fori_loop(0, LOCAL_HEADS, heads, 0)
    w_steps(LOCAL_HEADS)
    pass_on(LOCAL_HEADS - 1, 0)

    def attended_wait(hh, carry):
        got(at.at[feats(zl, hh), theirs], aor.at[hh])
        got(at.at[feats(1 - zl, hh), theirs], afr.at[hh])
        return carry
    lax.fori_loop(0, LOCAL_HEADS, attended_wait, 0)

    def pair_share(hh, carry):
        got(at.at[feats(zl, hh), pair_mine], por.at[hh])
        pair_share_copy(hh, zl).start()
        got(at.at[feats(1 - zl, hh), pair_mine], par.at[hh])
        pair_share_copy(hh, 1 - zl).start()
        return carry

    def pair_wait(hh, carry):
        for which in range(2):
            got(at.at[feats(which, hh), pair_theirs], pfr.at[hh, which])
        return carry

    def past(i, k):
        return jnp.where(i >= k, 1, 0)

    def slot_of(i):
        return past(i, 2) - past(i, 4) + past(i, 5) - past(i, 7)

    def group_p(i):
        return past(i, 1) - past(i, 2) + past(i, 3) + past(i, 4) + past(i, 6)

    def group_of(i):
        return zh_of(group_p(i))

    def zh_of(p):
        is1 = (p % 2) * (1 - p // 2)
        is2 = (1 - p % 2) * (p // 2)
        is3 = (p % 2) * (p // 2)
        return (zh + 4 - sgn * is1 + sgn * is2 + 2 * is3) % 4

    def lane_block(xx):
        return pl.ds(al(xx * 128, 128), 128)

    def far_copies(i):
        yield rc(far_out.at[i, pl.ds(0, WC), :], far_in.at[i, 0], ffs.at[i, 0], ffr.at[i, 0],
                 dev(xp, y, z, c))
        yield rc(far_out.at[i, pl.ds(WC, WC), :], far_in.at[i, 1], ffs.at[i, 1], ffr.at[i, 1],
                 dev(xm, y, z, c))

    def near_copies(i):
        yield rc(near_out.at[i, 0], near_in.at[i, 0], nns.at[i, 0], nnr.at[i, 0], dev(xp, y, z, c))
        yield rc(near_out.at[i, 1], near_in.at[i, 1], nns.at[i, 1], nnr.at[i, 1], dev(xm, y, z, c))

    def stage_a(i):
        rows = pl.ds(al(group_of(i) * GC, 32), GC)
        lanes = pl.ds(al(slot_of(i) * 512, 128), 512)
        pf[i] = jnp.dot(wt[rows, :], at[:, lanes], preferred_element_type=F32)
        far_out[i] = pf[i, :, lane_block((x + 2) % NX)].astype(BF)
        for cp in far_copies(i):
            cp.start()

    def stage_b(i):
        for d in range(2):
            got(far_in.at[i, d], ffr.at[i, d])
        up = lane_block(xp)
        down = lane_block(xm)
        lo, hi = pl.ds(0, WC), pl.ds(WC, WC)
        near_out[i, 0, lo, :] = (pf[i, lo, up] + far_in[i, 0].astype(F32)).astype(BF)
        near_out[i, 0, hi, :] = pf[i, hi, up].astype(BF)
        near_out[i, 1, lo, :] = pf[i, lo, down].astype(BF)
        near_out[i, 1, hi, :] = (pf[i, hi, down] + far_in[i, 1].astype(F32)).astype(BF)
        for cp in near_copies(i):
            cp.start()

    def stage_c(i):
        for d in range(2):
            got(near_in.at[i, d], nnr.at[i, d])
        rows = pl.ds(al(group_of(i) * GC, 32), GC)
        total = (pf[i, :, lane_block(x)] + near_in[i, 0].astype(F32)
                 + near_in[i, 1].astype(F32))
        whose = slot_of(i)

        @pl.when(whose == 0)
        def _():
            ft[rows, :] = total

        @pl.when(whose == 1)
        def _():
            pair_out[rows, :] = (total * gate_col[rows, :]).astype(BF)
            pair_sum(group_p(i)).start()

    def pair_sum(p):
        rows = pl.ds(al(zh_of(p) * GC, 32), GC)
        return rc(pair_out.at[rows, :], pair_in.at[rows, :], pss.at[p], psr.at[p], pair)

    def inputs_sent():
        for hh in range(LOCAL_HEADS - AHEAD, LOCAL_HEADS):
            head_sent(hh)

        def head_passed(hh, carry):
            @pl.when(jnp.logical_not(q_stays))
            def _():
                q_copy(head, hh, qos.at[hh]).wait_send()
            kv_pass(hh).wait_send()
            return carry
        lax.fori_loop(0, LOCAL_HEADS, head_passed, 0)

        def heads_sent(hh, carry):
            away_copy(hh).wait_send()
            home_copy(hh).wait_send()
            pass_copy(hh).wait_send()
            pair_home_copy(hh).wait_send()
            pair_pass_copy(hh).wait_send()
            for which in range(2):
                pair_share_copy(hh, which).wait_send()
            return carry
        lax.fori_loop(0, LOCAL_HEADS, heads_sent, 0)

    def weights_sent():
        @pl.when(jnp.logical_not(is_row_core))
        def _():
            rc(w_own, piece(z, c), w0s, w0r.at[c], other).wait_send()

        @pl.when(is_row_core)
        def _():
            for d in range(2):
                for k in range(1, 4):
                    z_send(d, k).wait_send()

                @pl.when(d == 1 - zl)
                def _(d=d):
                    z_send(d, 4).wait_send()
            row_send(z, 0).wait_send()
            for k in range(1, 4):
                for d in range(2):
                    row_send(z_from(d, k), z_index(d, k)).wait_send()
            row_send((z + 4) % NZ, 7).wait_send()

    def sums_sent(i):
        for cp in far_copies(i):
            cp.wait_send()
        for cp in near_copies(i):
            cp.wait_send()

    def step(i, carry):
        for p, when in enumerate((0, 1, 4, 6)):
            @pl.when(i == when)
            def _(p=p):
                row_wait(p)

        @pl.when(i == 1)
        def _():
            lax.fori_loop(0, LOCAL_HEADS, pair_share, 0)

        @pl.when(i == 2)
        def _():
            lax.fori_loop(0, LOCAL_HEADS, pair_wait, 0)

        @pl.when(i < GROUPS)
        def _():
            stage_a(i)

        @pl.when(jnp.logical_and(i >= NEAR_LAG, i < GROUPS + NEAR_LAG))
        def _():
            stage_b(i - NEAR_LAG)

        @pl.when(i >= LAST_LAG)
        def _():
            stage_c(i - LAST_LAG)
        w_steps(i, 10)

        @pl.when(i == 5)
        def _():
            inputs_sent()

        @pl.when(i == GROUPS + LAST_LAG - 2)
        def _():
            weights_sent()

        @pl.when(i >= LAST_LAG + 1)
        def _():
            sums_sent(i - LAST_LAG - 1)
        return carry
    def tokens(which, cc):
        return ob.at[which, pl.ds(al(cc * TOK, TOK), TOK), :]

    def out_cols(row):
        return out_hbm.at[0, :, pl.ds(al(row * 1280, 128), 1280)]

    keep = [pltpu.make_async_copy(tokens(i, c), out_cols(row), fink.at[i])
            for i, row in enumerate((my_row, pair_row))]
    give = [rc(tokens(i, oc), out_cols(row), fins.at[i], finr.at[i], other)
            for i, row in enumerate((my_row, pair_row))]
    lax.fori_loop(0, GROUPS + LAST_LAG - 1, step, 0)
    stage_c(GROUPS - 1)
    for b in range(10):
        here = slice(b * 128, b * 128 + 128)
        ob[0, :, here] = (ft[here, :].T * gate_row[0, :, here]).astype(BF)
    keep[0].start()
    give[0].start()
    for p in range(4):
        got(pair_in.at[pl.ds(al(zh_of(p) * GC, 32), GC), :], psr.at[p])
    for b in range(10):
        here = slice(b * 128, b * 128 + 128)
        ob[1, :, here] = pair_in[here, :].T
    keep[1].start()
    give[1].start()

    for i in range(GROUPS - 2, GROUPS):
        sums_sent(i)
    gate_copy.wait_send()
    for p in range(4):
        pair_sum(p).wait_send()
    for i, yy in enumerate((y, y_pair)):
        keep[i].wait()
        give[i].wait_send()
        differs = (oc - yy % 2) * (oc - yy % 2)
        got(out_cols((1 - differs) * yy + differs * (3 - yy)), finr.at[i])


def body(query_rows, key_rows, value_rows, query_gain, key_gain, out_weight, gate_table, lengths,
         step_index):
    smem = pl.BlockSpec(memory_space=pltpu.SMEM)
    hbm = pl.BlockSpec(memory_space=pl.ANY)
    sem = pltpu.SemaphoreType.DMA
    flops = 2 * (2 * 5 * 512 * 1024 * 128 + 512 * 1280 * 2560)
    return pl.pallas_call(
        kernel,
        out_shape=jax.ShapeDtypeStruct((1, TOK, D), BF),
        in_specs=[smem, smem] + [hbm] * 7,
        out_specs=hbm,
        scratch_shapes=[
            pltpu.VMEM((1, D), F32),
            pltpu.VMEM((1, D), F32),
            pltpu.VMEM((TOK, D), BF),
            pltpu.VMEM((TOK, D), BF),
            pltpu.VMEM((TOK, D), BF),
            pltpu.VMEM((TOK, D), BF),
            pltpu.VMEM((TOK, 2 * D), BF),
            pltpu.VMEM((WC, GW), BF),
            pltpu.VMEM((2, STEPS, 1280), F32),
            pltpu.VMEM((3, 1, 1280), F32),
            pltpu.VMEM((512, GW), BF),
            pltpu.VMEM((KEYS, 2 * GW), BF),
            pltpu.VMEM((KEYS, 128), F32),
            pltpu.VMEM((1280, 2 * GW), BF),
            pltpu.VMEM((LOCAL_HEADS, HD, 256), BF),
            pltpu.VMEM((2 * GW, 1024), BF),
            pltpu.VMEM((GROUPS, GC, 512), F32),
            pltpu.VMEM((GROUPS, GC, 128), BF),
            pltpu.VMEM((GROUPS, 2, WC, 128), BF),
            pltpu.VMEM((GROUPS, 2, GC, 128), BF),
            pltpu.VMEM((GROUPS, 2, GC, 128), BF),
            pltpu.VMEM((1280, 128), F32),
            pltpu.VMEM((1280, 128), F32),
            pltpu.VMEM((1280, 128), BF),
            pltpu.VMEM((1280, 128), BF),
            pltpu.VMEM((2, 128, 1280), BF),
            sem((8,)),
            sem, sem,
            sem((5,)), sem((5,)), sem((5,)), sem((5,)), sem((5,)),
            sem((5,)), sem((5,)),
            sem, sem((2,)),
            sem((2, 4)), sem((2, 4)),
            sem((8,)), sem((8,)),
            sem((5,)), sem((5,)), sem((5,)), sem((5,)), sem((5,)), sem((5,)),
            sem((5,)), sem((5,)), sem((5,)), sem((5,)), sem((5, 2)), sem((5, 2)),
            sem((8, 2)), sem((8, 2)), sem((8, 2)), sem((8, 2)),
            sem((4,)), sem((4,)),
            sem((2,)), sem((2,)), sem((2,)),
        ],
        compiler_params=pltpu.CompilerParams(
            collective_id=0, has_side_effects=True, vmem_limit_bytes=60 * 2**20),
        cost_estimate=pl.CostEstimate(flops=flops, bytes_accessed=4 * 2**20,
                                      transcendentals=5 * 512 * 1024),
        name="gated_attention",
    )(lengths, step_index, query_rows, key_rows, value_rows, query_gain[None], key_gain[None],
      out_weight.T, gate_table)


def solution(mesh):
    placed = (
        P("slot", ("head", "blk"), None),
        P("slot", ("head", "blk"), None),
        P("slot", ("head", "blk"), None),
        P(),
        P(),
        P("head", ("slot", "blk")),
        P(),
        P("slot"),
        P("slot"),
    )
    return jax.shard_map(
        body,
        mesh=mesh,
        in_specs=placed,
        out_specs=P("slot", ("head", "blk"), None),
        check_vma=False,
    )
```

```python
import functools
import math

import jax
import jax.numpy as jnp
from jax import lax
from jax.experimental import pallas as pl
from jax.experimental.pallas import tpu as pltpu
from jax.sharding import PartitionSpec as P

HD = 128
NEG_BIG = -1e30
EPSILON = 1e-06
MESH = pl.DeviceIdType.MESH

NX, NY, NZ, NC = 4, 4, 8, 2
TOK = 64
D = 5120
GW = 640
LOCAL_HEADS = GW // HD
KEYS = 1024
WC = 160
GC = 2 * WC
GROUPS = 8
AHEAD = 2
W_STEPS = ((-1, 1), (1, 1), (-2, 3), (2, 3), (-3, 5), (3, 5), (-4, 13))
NEAR_LAG = 2
LAST_LAG = 4
STEPS = 50
BF = jnp.bfloat16
F32 = jnp.float32


def al(value, unit):
    return pl.multiple_of(value, unit)


def kernel(
    len_ref, step_ref, q_hbm, k_hbm, v_hbm, qg_hbm, kg_hbm, w_hbm, gt_hbm, out_hbm,
    qg_ref, kg_ref, q_raw, k_raw, v_raw, q_nrm, kv_nrm, w_own, gate_tab,
    gate_row, qb, kvb, bias, wt,
    a_stage, at, pf, far_out, far_in, near_out, near_in, ft, gate_col, pair_out, pair_in, ob,
    ld, gs, gr, qs, qr, qos, ks, kr, fs, fr, w0s, w0r, zs, zr, yds, ydr,
    azs, azr, aos, aor, afs, afr, pos, por, pas, par, pfs, pfr, ffs, ffr, nns, nnr, pss, psr, fins, finr, fink,
):
    slot = lax.axis_index("slot")
    head = lax.axis_index("head")
    c = lax.axis_index("blk")
    x, zl = head // 2, head % 2
    y, zh = slot // 4, slot % 4
    z = zh * 2 + zl
    oc = 1 - c
    row_core = y % 2
    is_row_core = c == row_core
    y_pair = y + 1 - 2 * (y % 2)
    y_row = 3 - y

    def row_of(yy):
        differs = (c - yy % 2) * (c - yy % 2)
        return (1 - differs) * yy + differs * (3 - yy)
    my_row = row_of(y)
    pair_row = row_of(y_pair)

    def dev(dx, dy, dz, dc):
        return (dy * 4 + dz // 2, dx * 2 + dz % 2, dc)

    def rc(src, dst, send, recv, device):
        return pltpu.make_async_remote_copy(
            src_ref=src, dst_ref=dst, send_sem=send, recv_sem=recv,
            device_id=device, device_id_type=MESH,
        )

    def got(ref, sem):
        pltpu.make_async_copy(ref, ref, sem).wait()

    xp, xm = (x + 1) % NX, (x + 3) % NX
    zp, zm = (z + 1) % NZ, (z + 7) % NZ
    z_mate = zh * 2 + (1 - zl)
    z_out = (z + NZ - 1 + 2 * zl) % NZ
    other = dev(x, y, z, oc)
    pair = dev(x, y_pair, z, c)

    load_w = pltpu.make_async_copy(w_hbm, w_own, ld.at[0])
    load_k = pltpu.make_async_copy(k_hbm.at[0], k_raw, ld.at[1])
    load_q = pltpu.make_async_copy(q_hbm.at[0], q_raw, ld.at[2])
    load_g = [
        pltpu.make_async_copy(
            gt_hbm.at[:, pl.ds(al(row * 1280, 128), 1280)], gate_tab.at[i], ld.at[3 + i])
        for i, row in enumerate((my_row, pair_row))
    ]
    load_kg = pltpu.make_async_copy(kg_hbm, kg_ref, ld.at[5])
    load_qg = pltpu.make_async_copy(qg_hbm, qg_ref, ld.at[6])
    load_v = pltpu.make_async_copy(v_hbm.at[0], v_raw, ld.at[7])
    load_w.start()
    load_v.start()
    load_k.start()
    load_kg.start()
    load_qg.start()
    load_q.start()
    for cp in load_g:
        cp.start()

    barrier = pltpu.get_barrier_semaphore()
    partners = []
    for dh in range(8):
        for dc in range(2):
            if (dh, dc) != (0, 0):
                ph = (head + dh) % 8
                partners.append((slot, ph, (c + dc) % 2))
    partners.append(dev(x, y, z_out, c))
    partners.append(dev(x, y_row, z, c))
    partners.append(pair)
    partners.append(dev(x, y_pair, z, oc))
    for partner in partners:
        pl.semaphore_signal(barrier, inc=1, device_id=partner, device_id_type=MESH)

    def cols(ref, group):
        return ref.at[:, pl.ds(al(group * GW, 128), GW)]

    def kv_lanes(hh):
        return pl.ds(al(hh * 2 * HD, 2 * HD), 2 * HD)

    def q_lanes(hh):
        return pl.ds(al(hh * HD, HD), HD)

    def kv_place(hh):
        return kvb.at[pl.ds(al(c * 512 + head * TOK, TOK), TOK), kv_lanes(hh)]

    def kv_part(group, hh):
        return kv_nrm.at[:, pl.ds(al(group * 2 * GW + hh * 2 * HD, 2 * HD), 2 * HD)]

    def kv_half(which_c, hh):
        return kvb.at[pl.ds(al(which_c * 512, 512), 512), kv_lanes(hh)]

    def kv_pass(hh):
        ref = kv_half(c, hh)
        return rc(ref, ref, fs.at[hh], fr.at[hh], other)

    q_core = x // 2
    q_stays = c == q_core
    q_row = zl * 256 + (x % 2) * 128 + c * TOK

    def q_place(hh):
        return qb.at[pl.ds(al(q_row, TOK), TOK), q_lanes(hh)]

    def q_part(group, hh):
        return q_nrm.at[:, pl.ds(al(group * GW + hh * HD, HD), HD)]

    def q_copy(group, hh, send):
        return rc(q_part(group, hh), q_place(hh), send, qr.at[hh], (slot, group, q_core))

    def send_head(hh):
        pltpu.make_async_copy(kv_part(head, hh), kv_place(hh), kr.at[hh]).start()

        @pl.when(q_stays)
        def _():
            pltpu.make_async_copy(q_part(head, hh), q_place(hh), qr.at[hh]).start()

        @pl.when(jnp.logical_not(q_stays))
        def _():
            q_copy(head, hh, qos.at[hh]).start()

        def one(t, carry):
            group = (head + t) % 8
            rc(kv_part(group, hh), kv_place(hh), ks.at[hh], kr.at[hh], (slot, group, c)).start()
            q_copy(group, hh, qs.at[hh]).start()
            return carry
        lax.fori_loop(1, 8, one, 0)

    def head_sent(hh):
        got(kvb.at[pl.ds(0, 7 * TOK), kv_lanes(hh)], ks.at[hh])
        got(qb.at[pl.ds(0, 7 * TOK), q_lanes(hh)], qs.at[hh])

    def head_here(hh):
        got(kv_half(c, hh), kr.at[hh])
        kv_pass(hh).start()
        got(qb.at[:, q_lanes(hh)], qr.at[hh])
        got(kv_half(oc, hh), fr.at[hh])

    def piece(zsrc, half=None):
        row = (zsrc // 2) * GC
        size = GC
        if half is not None:
            row = row + half * WC
            size = WC
        return wt.at[pl.ds(al(row, 32), size), pl.ds(al((zsrc % 2) * GW, 128), GW)]

    def row_send(zsrc, j):
        return rc(piece(zsrc), piece(zsrc), yds.at[j], ydr.at[j], dev(x, y_row, z, c))

    def z_send(d, k):
        zsrc = (z + NZ - (k - 1)) % NZ if d == 0 else (z + k - 1) % NZ
        return rc(piece(zsrc), piece(zsrc), zs.at[d, k - 1], zr.at[d, k - 1],
                  dev(x, y, zp if d == 0 else zm, c))

    def z_from(d, k):
        return (z + NZ - k) % NZ if d == 0 else (z + k) % NZ

    def z_index(d, k):
        ahead = zl if d == 0 else 1 - zl
        if k == 1:
            return 2 - ahead
        if k == 2:
            return 3 + ahead
        return 6 - ahead

    def z_first():
        @pl.when(is_row_core)
        def _():
            got(piece(z, 0), w0r.at[0])
            got(piece(z, 1), w0r.at[1])
            for d in range(2):
                z_send(d, 1).start()
            row_send(z, 0).start()

    def z_take(k):
        @pl.when(is_row_core)
        def _():
            for d in range(2):
                zsrc = z_from(d, k)
                got(piece(zsrc), zr.at[d, k - 1])
                row_send(zsrc, z_index(d, k)).start()

    def z_on(k):
        @pl.when(is_row_core)
        def _():
            for d in range(2):
                if k < 3:
                    z_send(d, k + 1).start()
                else:
                    @pl.when(d == 1 - zl)
                    def _(d=d):
                        z_send(d, 4).start()

    def z_last():
        @pl.when(is_row_core)
        def _():
            zsrc = (z + 4) % NZ
            got(piece(zsrc), zr.at[zl, 3])
            row_send(zsrc, 7).start()

    sgn = 1 - 2 * zl
    DELTA = (0, 1, -1, -2, 2, 3, -3, 4)

    def z_of(j):
        return (z + NZ + sgn * DELTA[j]) % NZ

    def row_wait(p):
        @pl.when(jnp.logical_not(is_row_core))
        def _():
            for j in (2 * p, 2 * p + 1):
                got(piece(z_of(j)), ydr.at[j])

    def normed(raw, gain_ref, here):
        vals = raw[here, :].astype(F32)
        mean_square = jnp.mean(vals * vals, axis=-1, keepdims=True)
        return (vals * lax.rsqrt(mean_square + EPSILON) * gain_ref[...]).astype(BF)

    def kv_rows(i, carry):
        here = pl.ds(al(i * 16, 16), 16)
        out = normed(k_raw, kg_ref, here)
        for hh in range(D // HD):
            src = slice(hh * HD, hh * HD + HD)
            kv_nrm[here, hh * 2 * HD:hh * 2 * HD + HD] = out[:, src]
            kv_nrm[here, hh * 2 * HD + HD:hh * 2 * HD + 2 * HD] = v_raw[here, src]
        return carry

    def q_rows(i, carry):
        here = pl.ds(al(i * 16, 16), 16)
        q_nrm[here, :] = normed(q_raw, qg_ref, here)
        return carry

    load_k.wait()
    load_kg.wait()
    load_v.wait()
    lax.fori_loop(0, TOK // 16, kv_rows, 0)
    load_q.wait()
    load_qg.wait()
    lax.fori_loop(0, TOK // 16, q_rows, 0)

    pl.semaphore_wait(barrier, len(partners))
    load_w.wait()

    @pl.when(is_row_core)
    def _():
        pltpu.make_async_copy(w_own, piece(z, c), w0r.at[c]).start()

    @pl.when(jnp.logical_not(is_row_core))
    def _():
        rc(w_own, piece(z, c), w0s, w0r.at[c], other).start()

    for hh in range(AHEAD):
        send_head(hh)
    z_first()

    def mask_rows(i, carry):
        row = lax.broadcasted_iota(jnp.int32, (TOK, 128), 0)
        pos = (i % 8) * 128 + (i // 8) * TOK + row
        bias[pl.ds(al(i * TOK, TOK), TOK), :] = jnp.where(pos < len_ref[0], 0.0, NEG_BIG)
        return carry
    lax.fori_loop(0, KEYS // TOK, mask_rows, 0)

    step_rows = lax.broadcasted_iota(jnp.int32, (STEPS, 1280), 0)
    for i in range(2):
        load_g[i].wait()
        gate_row[i] = jnp.sum(
            jnp.where(step_rows == step_ref[0], gate_tab[i], 0.0), axis=0, keepdims=True)
    gate_copy = rc(gate_row.at[1], gate_row.at[2], gs, gr, pair)
    gate_copy.start()

    got(gate_row.at[2], gr)
    gate_col[...] = jnp.broadcast_to(gate_row[2], (128, 1280)).T

    scale = math.log2(math.e) / math.sqrt(HD)
    mine = pl.ds(al(c * 256, 128), 256)
    theirs = pl.ds(al(oc * 256, 128), 256)
    pair_mine = pl.ds(al(512 + c * 256, 128), 256)
    pair_theirs = pl.ds(al(512 + oc * 256, 128), 256)

    def feats(which_zl, hh):
        return pl.ds(al(which_zl * GW + hh * HD, HD), HD)

    def attend(hh, zq):
        lanes = q_lanes(hh)
        keys = kvb[:, pl.ds(al(hh * 2 * HD, HD), HD)]
        values = kvb[:, pl.ds(al(hh * 2 * HD + HD, HD), HD)]
        queries = qb[pl.ds(al(zq * 256, 256), 256), lanes]
        scores = lax.dot_general(keys, queries, (((1,), (1,)), ((), ())),
                                 preferred_element_type=F32)
        scores = scores * scale + jnp.concatenate([bias[...], bias[...]], axis=1)
        top = jnp.max(scores, axis=0, keepdims=True)
        weights = jnp.exp2(scores - top)
        total = jnp.sum(weights, axis=0, keepdims=True)
        mixed = lax.dot_general(values, weights.astype(BF), (((0,), (0,)), ((), ())),
                                preferred_element_type=F32)
        return (mixed / total).astype(BF)

    def away_copy(hh):
        return rc(a_stage.at[hh], at.at[feats(zl, hh), mine], azs.at[hh], azr.at[hh],
                  dev(x, y, z_mate, c))

    def home_copy(hh):
        ref = at.at[feats(zl, hh), mine]
        return rc(ref, ref, aos.at[hh], aor.at[hh], other)

    def pass_copy(hh):
        ref = at.at[feats(1 - zl, hh), mine]
        return rc(ref, ref, afs.at[hh], afr.at[hh], other)

    def pair_home_copy(hh):
        return rc(at.at[feats(zl, hh), mine], at.at[feats(zl, hh), pair_mine],
                  pos.at[hh], por.at[hh], pair)

    def pair_pass_copy(hh):
        return rc(at.at[feats(1 - zl, hh), mine], at.at[feats(1 - zl, hh), pair_mine],
                  pas.at[hh], par.at[hh], pair)

    def pair_share_copy(hh, which):
        ref = at.at[feats(which, hh), pair_mine]
        return rc(ref, ref, pfs.at[hh, which], pfr.at[hh, which], other)

    def one_head(hh):
        a_stage[hh] = attend(hh, 1 - zl)
        away_copy(hh).start()
        at[feats(zl, hh), mine] = attend(hh, zl)
        pair_home_copy(hh).start()
        home_copy(hh).start()

    def pass_on(hh, carry):
        got(at.at[feats(1 - zl, hh), mine], azr.at[hh])
        pair_pass_copy(hh).start()
        pass_copy(hh).start()
        return carry

    def w_steps(hh, first=0):
        for k, when in W_STEPS:
            if first <= when < first + 10:
                @pl.when(hh == when - first)
                def _(k=k):
                    if k == -4:
                        z_last()
                    else:
                        z_take(-k) if k < 0 else z_on(k)

    def heads(hh, carry):
        @pl.when(hh + AHEAD < LOCAL_HEADS)
        def _():
            head_sent(hh)
            send_head(hh + AHEAD)
        head_here(hh)
        one_head(hh)
        w_steps(hh)

        @pl.when(hh > 0)
        def _():
            pass_on(hh - 1, 0)
        return carry
    lax.fori_loop(0, LOCAL_HEADS, heads, 0)
    w_steps(LOCAL_HEADS)
    pass_on(LOCAL_HEADS - 1, 0)

    def attended_wait(hh, carry):
        got(at.at[feats(zl, hh), theirs], aor.at[hh])
        got(at.at[feats(1 - zl, hh), theirs], afr.at[hh])
        return carry
    lax.fori_loop(0, LOCAL_HEADS, attended_wait, 0)

    def pair_share(hh, carry):
        got(at.at[feats(zl, hh), pair_mine], por.at[hh])
        pair_share_copy(hh, zl).start()
        got(at.at[feats(1 - zl, hh), pair_mine], par.at[hh])
        pair_share_copy(hh, 1 - zl).start()
        return carry

    def pair_wait(hh, carry):
        for which in range(2):
            got(at.at[feats(which, hh), pair_theirs], pfr.at[hh, which])
        return carry

    def past(i, k):
        return jnp.where(i >= k, 1, 0)

    def slot_of(i):
        return past(i, 2) - past(i, 4) + past(i, 5) - past(i, 7)

    def group_p(i):
        return past(i, 1) - past(i, 2) + past(i, 3) + past(i, 4) + past(i, 6)

    def group_of(i):
        return zh_of(group_p(i))

    def zh_of(p):
        is1 = (p % 2) * (1 - p // 2)
        is2 = (1 - p % 2) * (p // 2)
        is3 = (p % 2) * (p // 2)
        return (zh + 4 - sgn * is1 + sgn * is2 + 2 * is3) % 4

    def lane_block(xx):
        return pl.ds(al(xx * 128, 128), 128)

    def far_copies(i):
        yield rc(far_out.at[i, pl.ds(0, WC), :], far_in.at[i, 0], ffs.at[i, 0], ffr.at[i, 0],
                 dev(xp, y, z, c))
        yield rc(far_out.at[i, pl.ds(WC, WC), :], far_in.at[i, 1], ffs.at[i, 1], ffr.at[i, 1],
                 dev(xm, y, z, c))

    def near_copies(i):
        yield rc(near_out.at[i, 0], near_in.at[i, 0], nns.at[i, 0], nnr.at[i, 0], dev(xp, y, z, c))
        yield rc(near_out.at[i, 1], near_in.at[i, 1], nns.at[i, 1], nnr.at[i, 1], dev(xm, y, z, c))

    def stage_a(i):
        rows = pl.ds(al(group_of(i) * GC, 32), GC)
        lanes = pl.ds(al(slot_of(i) * 512, 128), 512)
        pf[i] = jnp.dot(wt[rows, :], at[:, lanes], preferred_element_type=F32)
        far_out[i] = pf[i, :, lane_block((x + 2) % NX)].astype(BF)
        for cp in far_copies(i):
            cp.start()

    def stage_b(i):
        for d in range(2):
            got(far_in.at[i, d], ffr.at[i, d])
        up = lane_block(xp)
        down = lane_block(xm)
        lo, hi = pl.ds(0, WC), pl.ds(WC, WC)
        near_out[i, 0, lo, :] = (pf[i, lo, up] + far_in[i, 0].astype(F32)).astype(BF)
        near_out[i, 0, hi, :] = pf[i, hi, up].astype(BF)
        near_out[i, 1, lo, :] = pf[i, lo, down].astype(BF)
        near_out[i, 1, hi, :] = (pf[i, hi, down] + far_in[i, 1].astype(F32)).astype(BF)
        for cp in near_copies(i):
            cp.start()

    def stage_c(i):
        for d in range(2):
            got(near_in.at[i, d], nnr.at[i, d])
        rows = pl.ds(al(group_of(i) * GC, 32), GC)
        total = (pf[i, :, lane_block(x)] + near_in[i, 0].astype(F32)
                 + near_in[i, 1].astype(F32))
        whose = slot_of(i)

        @pl.when(whose == 0)
        def _():
            ft[rows, :] = total

        @pl.when(whose == 1)
        def _():
            pair_out[rows, :] = (total * gate_col[rows, :]).astype(BF)
            pair_sum(group_p(i)).start()

    def pair_sum(p):
        rows = pl.ds(al(zh_of(p) * GC, 32), GC)
        return rc(pair_out.at[rows, :], pair_in.at[rows, :], pss.at[p], psr.at[p], pair)

    def inputs_sent():
        for hh in range(LOCAL_HEADS - AHEAD, LOCAL_HEADS):
            head_sent(hh)

        def head_passed(hh, carry):
            @pl.when(jnp.logical_not(q_stays))
            def _():
                q_copy(head, hh, qos.at[hh]).wait_send()
            kv_pass(hh).wait_send()
            return carry
        lax.fori_loop(0, LOCAL_HEADS, head_passed, 0)

        def heads_sent(hh, carry):
            away_copy(hh).wait_send()
            home_copy(hh).wait_send()
            pass_copy(hh).wait_send()
            pair_home_copy(hh).wait_send()
            pair_pass_copy(hh).wait_send()
            for which in range(2):
                pair_share_copy(hh, which).wait_send()
            return carry
        lax.fori_loop(0, LOCAL_HEADS, heads_sent, 0)

    def weights_sent():
        @pl.when(jnp.logical_not(is_row_core))
        def _():
            rc(w_own, piece(z, c), w0s, w0r.at[c], other).wait_send()

        @pl.when(is_row_core)
        def _():
            for d in range(2):
                for k in range(1, 4):
                    z_send(d, k).wait_send()

                @pl.when(d == 1 - zl)
                def _(d=d):
                    z_send(d, 4).wait_send()
            row_send(z, 0).wait_send()
            for k in range(1, 4):
                for d in range(2):
                    row_send(z_from(d, k), z_index(d, k)).wait_send()
            row_send((z + 4) % NZ, 7).wait_send()

    def sums_sent(i):
        for cp in far_copies(i):
            cp.wait_send()
        for cp in near_copies(i):
            cp.wait_send()

    def step(i, carry):
        for p, when in enumerate((0, 1, 4, 6)):
            @pl.when(i == when)
            def _(p=p):
                row_wait(p)

        @pl.when(i == 1)
        def _():
            lax.fori_loop(0, LOCAL_HEADS, pair_share, 0)

        @pl.when(i == 2)
        def _():
            lax.fori_loop(0, LOCAL_HEADS, pair_wait, 0)

        @pl.when(i < GROUPS)
        def _():
            stage_a(i)

        @pl.when(jnp.logical_and(i >= NEAR_LAG, i < GROUPS + NEAR_LAG))
        def _():
            stage_b(i - NEAR_LAG)

        @pl.when(i >= LAST_LAG)
        def _():
            stage_c(i - LAST_LAG)
        w_steps(i, 10)

        @pl.when(i == 5)
        def _():
            inputs_sent()

        @pl.when(i == GROUPS + LAST_LAG - 2)
        def _():
            weights_sent()

        @pl.when(i >= LAST_LAG + 1)
        def _():
            sums_sent(i - LAST_LAG - 1)
        return carry
    def tokens(which, cc):
        return ob.at[which, pl.ds(al(cc * TOK, TOK), TOK), :]

    def out_cols(row):
        return out_hbm.at[0, :, pl.ds(al(row * 1280, 128), 1280)]

    keep = [pltpu.make_async_copy(tokens(i, c), out_cols(row), fink.at[i])
            for i, row in enumerate((my_row, pair_row))]
    give = [rc(tokens(i, oc), out_cols(row), fins.at[i], finr.at[i], other)
            for i, row in enumerate((my_row, pair_row))]
    lax.fori_loop(0, GROUPS + LAST_LAG - 1, step, 0)
    stage_c(GROUPS - 1)
    for b in range(10):
        here = slice(b * 128, b * 128 + 128)
        ob[0, :, here] = (ft[here, :].T * gate_row[0, :, here]).astype(BF)
    keep[0].start()
    give[0].start()
    for p in range(4):
        got(pair_in.at[pl.ds(al(zh_of(p) * GC, 32), GC), :], psr.at[p])
    for b in range(10):
        here = slice(b * 128, b * 128 + 128)
        ob[1, :, here] = pair_in[here, :].T
    keep[1].start()
    give[1].start()

    for i in range(GROUPS - 2, GROUPS):
        sums_sent(i)
    gate_copy.wait_send()
    for p in range(4):
        pair_sum(p).wait_send()
    for i, yy in enumerate((y, y_pair)):
        keep[i].wait()
        give[i].wait_send()
        differs = (oc - yy % 2) * (oc - yy % 2)
        got(out_cols((1 - differs) * yy + differs * (3 - yy)), finr.at[i])


def body(query_rows, key_rows, value_rows, query_gain, key_gain, out_weight, gate_table, lengths,
         step_index):
    smem = pl.BlockSpec(memory_space=pltpu.SMEM)
    hbm = pl.BlockSpec(memory_space=pl.ANY)
    sem = pltpu.SemaphoreType.DMA
    flops = 2 * (2 * 5 * 512 * 1024 * 128 + 512 * 1280 * 2560)
    return pl.pallas_call(
        kernel,
        out_shape=jax.ShapeDtypeStruct((1, TOK, D), BF),
        in_specs=[smem, smem] + [hbm] * 7,
        out_specs=hbm,
        scratch_shapes=[
            pltpu.VMEM((1, D), F32),
            pltpu.VMEM((1, D), F32),
            pltpu.VMEM((TOK, D), BF),
            pltpu.VMEM((TOK, D), BF),
            pltpu.VMEM((TOK, D), BF),
            pltpu.VMEM((TOK, D), BF),
            pltpu.VMEM((TOK, 2 * D), BF),
            pltpu.VMEM((WC, GW), BF),
            pltpu.VMEM((2, STEPS, 1280), F32),
            pltpu.VMEM((3, 1, 1280), F32),
            pltpu.VMEM((512, GW), BF),
            pltpu.VMEM((KEYS, 2 * GW), BF),
            pltpu.VMEM((KEYS, 128), F32),
            pltpu.VMEM((1280, 2 * GW), BF),
            pltpu.VMEM((LOCAL_HEADS, HD, 256), BF),
            pltpu.VMEM((2 * GW, 1024), BF),
            pltpu.VMEM((GROUPS, GC, 512), F32),
            pltpu.VMEM((GROUPS, GC, 128), BF),
            pltpu.VMEM((GROUPS, 2, WC, 128), BF),
            pltpu.VMEM((GROUPS, 2, GC, 128), BF),
            pltpu.VMEM((GROUPS, 2, GC, 128), BF),
            pltpu.VMEM((1280, 128), F32),
            pltpu.VMEM((1280, 128), F32),
            pltpu.VMEM((1280, 128), BF),
            pltpu.VMEM((1280, 128), BF),
            pltpu.VMEM((2, 128, 1280), BF),
            sem((8,)),
            sem, sem,
            sem((5,)), sem((5,)), sem((5,)), sem((5,)), sem((5,)),
            sem((5,)), sem((5,)),
            sem, sem((2,)),
            sem((2, 4)), sem((2, 4)),
            sem((8,)), sem((8,)),
            sem((5,)), sem((5,)), sem((5,)), sem((5,)), sem((5,)), sem((5,)),
            sem((5,)), sem((5,)), sem((5,)), sem((5,)), sem((5, 2)), sem((5, 2)),
            sem((8, 2)), sem((8, 2)), sem((8, 2)), sem((8, 2)),
            sem((4,)), sem((4,)),
            sem((2,)), sem((2,)), sem((2,)),
        ],
        compiler_params=pltpu.CompilerParams(
            collective_id=0, has_side_effects=True, vmem_limit_bytes=60 * 2**20),
        cost_estimate=pl.CostEstimate(flops=flops, bytes_accessed=4 * 2**20,
                                      transcendentals=5 * 512 * 1024),
        name="gated_attention",
    )(lengths, step_index, query_rows, key_rows, value_rows, query_gain[None], key_gain[None],
      out_weight.T, gate_table)


def solution(mesh):
    placed = (
        P("slot", ("head", "blk"), None),
        P("slot", ("head", "blk"), None),
        P("slot", ("head", "blk"), None),
        P(),
        P(),
        P("head", ("slot", "blk")),
        P(),
        P("slot"),
        P("slot"),
    )
    return jax.shard_map(
        body,
        mesh=mesh,
        in_specs=placed,
        out_specs=P("slot", ("head", "blk"), None),
        check_vma=False,
    )
```

```python
import functools
import math

import jax
import jax.numpy as jnp
from jax import lax
from jax.experimental import pallas as pl
from jax.experimental.pallas import tpu as pltpu
from jax.sharding import PartitionSpec as P

HD = 128
NEG_BIG = -1e30
EPSILON = 1e-06
MESH = pl.DeviceIdType.MESH

NX, NY, NZ, NC = 4, 4, 8, 2
TOK = 64
D = 5120
GW = 640
LOCAL_HEADS = GW // HD
KEYS = 1024
WC = 160
GC = 2 * WC
GROUPS = 8
AHEAD = 2
W_STEPS = ((-1, 1), (1, 1), (-2, 3), (2, 3), (-3, 5), (3, 5), (-4, 13))
NEAR_LAG = 2
LAST_LAG = 4
STEPS = 50
BF = jnp.bfloat16
F32 = jnp.float32


def al(value, unit):
    return pl.multiple_of(value, unit)


def kernel(
    len_ref, step_ref, q_hbm, k_hbm, v_hbm, qg_hbm, kg_hbm, w_hbm, gt_hbm, out_hbm,
    qg_ref, kg_ref, q_raw, k_raw, v_raw, q_nrm, kv_nrm, w_own, gate_tab,
    gate_row, qb, kvb, bias, wt,
    a_stage, at, pf, far_out, far_in, near_out, near_in, ft, gate_col, pair_out, pair_in, ob,
    ld, gs, gr, qs, qr, qos, ks, kr, fs, fr, w0s, w0r, zs, zr, yds, ydr,
    azs, azr, aos, aor, afs, afr, pos, por, pas, par, pfs, pfr, ffs, ffr, nns, nnr, pss, psr, fins, finr, fink,
):
    slot = lax.axis_index("slot")
    head = lax.axis_index("head")
    c = lax.axis_index("blk")
    x, zl = head // 2, head % 2
    y, zh = slot // 4, slot % 4
    z = zh * 2 + zl
    oc = 1 - c
    row_core = y % 2
    is_row_core = c == row_core
    y_pair = y + 1 - 2 * (y % 2)
    y_row = 3 - y

    def row_of(yy):
        differs = (c - yy % 2) * (c - yy % 2)
        return (1 - differs) * yy + differs * (3 - yy)
    my_row = row_of(y)
    pair_row = row_of(y_pair)

    def dev(dx, dy, dz, dc):
        return (dy * 4 + dz // 2, dx * 2 + dz % 2, dc)

    def rc(src, dst, send, recv, device):
        return pltpu.make_async_remote_copy(
            src_ref=src, dst_ref=dst, send_sem=send, recv_sem=recv,
            device_id=device, device_id_type=MESH,
        )

    def got(ref, sem):
        pltpu.make_async_copy(ref, ref, sem).wait()

    xp, xm = (x + 1) % NX, (x + 3) % NX
    zp, zm = (z + 1) % NZ, (z + 7) % NZ
    z_mate = zh * 2 + (1 - zl)
    z_out = (z + NZ - 1 + 2 * zl) % NZ
    other = dev(x, y, z, oc)
    pair = dev(x, y_pair, z, c)

    load_w = pltpu.make_async_copy(w_hbm, w_own, ld.at[0])
    load_k = pltpu.make_async_copy(k_hbm.at[0], k_raw, ld.at[1])
    load_q = pltpu.make_async_copy(q_hbm.at[0], q_raw, ld.at[2])
    load_g = [
        pltpu.make_async_copy(
            gt_hbm.at[:, pl.ds(al(row * 1280, 128), 1280)], gate_tab.at[i], ld.at[3 + i])
        for i, row in enumerate((my_row, pair_row))
    ]
    load_kg = pltpu.make_async_copy(kg_hbm, kg_ref, ld.at[5])
    load_qg = pltpu.make_async_copy(qg_hbm, qg_ref, ld.at[6])
    load_v = pltpu.make_async_copy(v_hbm.at[0], v_raw, ld.at[7])
    load_w.start()
    load_v.start()
    load_k.start()
    load_kg.start()
    load_qg.start()
    load_q.start()
    for cp in load_g:
        cp.start()

    barrier = pltpu.get_barrier_semaphore()
    partners = []
    for dh in range(8):
        for dc in range(2):
            if (dh, dc) != (0, 0):
                ph = (head + dh) % 8
                partners.append((slot, ph, (c + dc) % 2))
    partners.append(dev(x, y, z_out, c))
    partners.append(dev(x, y_row, z, c))
    partners.append(pair)
    partners.append(dev(x, y_pair, z, oc))
    for partner in partners:
        pl.semaphore_signal(barrier, inc=1, device_id=partner, device_id_type=MESH)

    def cols(ref, group):
        return ref.at[:, pl.ds(al(group * GW, 128), GW)]

    def kv_lanes(hh):
        return pl.ds(al(hh * 2 * HD, 2 * HD), 2 * HD)

    def q_lanes(hh):
        return pl.ds(al(hh * HD, HD), HD)

    def kv_place(hh):
        return kvb.at[pl.ds(al(c * 512 + head * TOK, TOK), TOK), kv_lanes(hh)]

    def kv_part(group, hh):
        return kv_nrm.at[:, pl.ds(al(group * 2 * GW + hh * 2 * HD, 2 * HD), 2 * HD)]

    def kv_half(which_c, hh):
        return kvb.at[pl.ds(al(which_c * 512, 512), 512), kv_lanes(hh)]

    def kv_pass(hh):
        ref = kv_half(c, hh)
        return rc(ref, ref, fs.at[hh], fr.at[hh], other)

    q_core = x // 2
    q_stays = c == q_core
    q_row = zl * 256 + (x % 2) * 128 + c * TOK

    def q_place(hh):
        return qb.at[pl.ds(al(q_row, TOK), TOK), q_lanes(hh)]

    def q_part(group, hh):
        return q_nrm.at[:, pl.ds(al(group * GW + hh * HD, HD), HD)]

    def q_copy(group, hh, send):
        return rc(q_part(group, hh), q_place(hh), send, qr.at[hh], (slot, group, q_core))

    def send_head(hh):
        pltpu.make_async_copy(kv_part(head, hh), kv_place(hh), kr.at[hh]).start()

        @pl.when(q_stays)
        def _():
            pltpu.make_async_copy(q_part(head, hh), q_place(hh), qr.at[hh]).start()

        @pl.when(jnp.logical_not(q_stays))
        def _():
            q_copy(head, hh, qos.at[hh]).start()

        def one(t, carry):
            group = (head + t) % 8
            rc(kv_part(group, hh), kv_place(hh), ks.at[hh], kr.at[hh], (slot, group, c)).start()
            q_copy(group, hh, qs.at[hh]).start()
            return carry
        lax.fori_loop(1, 8, one, 0)

    def head_sent(hh):
        got(kvb.at[pl.ds(0, 7 * TOK), kv_lanes(hh)], ks.at[hh])
        got(qb.at[pl.ds(0, 7 * TOK), q_lanes(hh)], qs.at[hh])

    def head_here(hh):
        got(kv_half(c, hh), kr.at[hh])
        kv_pass(hh).start()
        got(qb.at[:, q_lanes(hh)], qr.at[hh])
        got(kv_half(oc, hh), fr.at[hh])

    def piece(zsrc, half=None):
        row = (zsrc // 2) * GC
        size = GC
        if half is not None:
            row = row + half * WC
            size = WC
        return wt.at[pl.ds(al(row, 32), size), pl.ds(al((zsrc % 2) * GW, 128), GW)]

    def row_send(zsrc, j):
        return rc(piece(zsrc), piece(zsrc), yds.at[j], ydr.at[j], dev(x, y_row, z, c))

    def z_send(d, k):
        zsrc = (z + NZ - (k - 1)) % NZ if d == 0 else (z + k - 1) % NZ
        return rc(piece(zsrc), piece(zsrc), zs.at[d, k - 1], zr.at[d, k - 1],
                  dev(x, y, zp if d == 0 else zm, c))

    def z_from(d, k):
        return (z + NZ - k) % NZ if d == 0 else (z + k) % NZ

    def z_index(d, k):
        ahead = zl if d == 0 else 1 - zl
        if k == 1:
            return 2 - ahead
        if k == 2:
            return 3 + ahead
        return 6 - ahead

    def z_first():
        @pl.when(is_row_core)
        def _():
            got(piece(z, 0), w0r.at[0])
            got(piece(z, 1), w0r.at[1])
            for d in range(2):
                z_send(d, 1).start()
            row_send(z, 0).start()

    def z_take(k):
        @pl.when(is_row_core)
        def _():
            for d in range(2):
                zsrc = z_from(d, k)
                got(piece(zsrc), zr.at[d, k - 1])
                row_send(zsrc, z_index(d, k)).start()

    def z_on(k):
        @pl.when(is_row_core)
        def _():
            for d in range(2):
                if k < 3:
                    z_send(d, k + 1).start()
                else:
                    @pl.when(d == 1 - zl)
                    def _(d=d):
                        z_send(d, 4).start()

    def z_last():
        @pl.when(is_row_core)
        def _():
            zsrc = (z + 4) % NZ
            got(piece(zsrc), zr.at[zl, 3])
            row_send(zsrc, 7).start()

    sgn = 1 - 2 * zl
    DELTA = (0, 1, -1, -2, 2, 3, -3, 4)

    def z_of(j):
        return (z + NZ + sgn * DELTA[j]) % NZ

    def row_wait(p):
        @pl.when(jnp.logical_not(is_row_core))
        def _():
            for j in (2 * p, 2 * p + 1):
                got(piece(z_of(j)), ydr.at[j])

    def normed(raw, gain_ref, here):
        vals = raw[here, :].astype(F32)
        mean_square = jnp.mean(vals * vals, axis=-1, keepdims=True)
        return (vals * lax.rsqrt(mean_square + EPSILON) * gain_ref[...]).astype(BF)

    def kv_rows(i, carry):
        here = pl.ds(al(i * 16, 16), 16)
        out = normed(k_raw, kg_ref, here)
        for hh in range(D // HD):
            src = slice(hh * HD, hh * HD + HD)
            kv_nrm[here, hh * 2 * HD:hh * 2 * HD + HD] = out[:, src]
            kv_nrm[here, hh * 2 * HD + HD:hh * 2 * HD + 2 * HD] = v_raw[here, src]
        return carry

    def q_rows(i, carry):
        here = pl.ds(al(i * 16, 16), 16)
        q_nrm[here, :] = normed(q_raw, qg_ref, here)
        return carry

    load_k.wait()
    load_kg.wait()
    load_v.wait()
    lax.fori_loop(0, TOK // 16, kv_rows, 0)
    load_q.wait()
    load_qg.wait()
    lax.fori_loop(0, TOK // 16, q_rows, 0)

    pl.semaphore_wait(barrier, len(partners))
    load_w.wait()

    @pl.when(is_row_core)
    def _():
        pltpu.make_async_copy(w_own, piece(z, c), w0r.at[c]).start()

    @pl.when(jnp.logical_not(is_row_core))
    def _():
        rc(w_own, piece(z, c), w0s, w0r.at[c], other).start()

    for hh in range(AHEAD):
        send_head(hh)
    z_first()

    def mask_rows(i, carry):
        row = lax.broadcasted_iota(jnp.int32, (TOK, 128), 0)
        pos = (i % 8) * 128 + (i // 8) * TOK + row
        bias[pl.ds(al(i * TOK, TOK), TOK), :] = jnp.where(pos < len_ref[0], 0.0, NEG_BIG)
        return carry
    lax.fori_loop(0, KEYS // TOK, mask_rows, 0)

    step_rows = lax.broadcasted_iota(jnp.int32, (STEPS, 1280), 0)
    for i in range(2):
        load_g[i].wait()
        gate_row[i] = jnp.sum(
            jnp.where(step_rows == step_ref[0], gate_tab[i], 0.0), axis=0, keepdims=True)
    gate_copy = rc(gate_row.at[1], gate_row.at[2], gs, gr, pair)
    gate_copy.start()

    got(gate_row.at[2], gr)
    gate_col[...] = jnp.broadcast_to(gate_row[2], (128, 1280)).T

    scale = math.log2(math.e) / math.sqrt(HD)
    mine = pl.ds(al(c * 256, 128), 256)
    theirs = pl.ds(al(oc * 256, 128), 256)
    pair_mine = pl.ds(al(512 + c * 256, 128), 256)
    pair_theirs = pl.ds(al(512 + oc * 256, 128), 256)

    def feats(which_zl, hh):
        return pl.ds(al(which_zl * GW + hh * HD, HD), HD)

    def attend(hh, zq):
        lanes = q_lanes(hh)
        keys = kvb[:, pl.ds(al(hh * 2 * HD, HD), HD)]
        values = kvb[:, pl.ds(al(hh * 2 * HD + HD, HD), HD)]
        queries = qb[pl.ds(al(zq * 256, 256), 256), lanes]
        scores = lax.dot_general(keys, queries, (((1,), (1,)), ((), ())),
                                 preferred_element_type=F32)
        scores = scores * scale + jnp.concatenate([bias[...], bias[...]], axis=1)
        top = jnp.max(scores, axis=0, keepdims=True)
        weights = jnp.exp2(scores - top)
        total = jnp.sum(weights, axis=0, keepdims=True)
        mixed = lax.dot_general(values, weights.astype(BF), (((0,), (0,)), ((), ())),
                                preferred_element_type=F32)
        return (mixed / total).astype(BF)

    def away_copy(hh):
        return rc(a_stage.at[hh], at.at[feats(zl, hh), mine], azs.at[hh], azr.at[hh],
                  dev(x, y, z_mate, c))

    def home_copy(hh):
        ref = at.at[feats(zl, hh), mine]
        return rc(ref, ref, aos.at[hh], aor.at[hh], other)

    def pass_copy(hh):
        ref = at.at[feats(1 - zl, hh), mine]
        return rc(ref, ref, afs.at[hh], afr.at[hh], other)

    def pair_home_copy(hh):
        return rc(at.at[feats(zl, hh), mine], at.at[feats(zl, hh), pair_mine],
                  pos.at[hh], por.at[hh], pair)

    def pair_pass_copy(hh):
        return rc(at.at[feats(1 - zl, hh), mine], at.at[feats(1 - zl, hh), pair_mine],
                  pas.at[hh], par.at[hh], pair)

    def pair_share_copy(hh, which):
        ref = at.at[feats(which, hh), pair_mine]
        return rc(ref, ref, pfs.at[hh, which], pfr.at[hh, which], other)

    def one_head(hh):
        a_stage[hh] = attend(hh, 1 - zl)
        away_copy(hh).start()
        at[feats(zl, hh), mine] = attend(hh, zl)
        pair_home_copy(hh).start()
        home_copy(hh).start()

    def pass_on(hh, carry):
        got(at.at[feats(1 - zl, hh), mine], azr.at[hh])
        pair_pass_copy(hh).start()
        pass_copy(hh).start()
        return carry

    def w_steps(hh, first=0):
        for k, when in W_STEPS:
            if first <= when < first + 10:
                @pl.when(hh == when - first)
                def _(k=k):
                    if k == -4:
                        z_last()
                    else:
                        z_take(-k) if k < 0 else z_on(k)

    def heads(hh, carry):
        @pl.when(hh + AHEAD < LOCAL_HEADS)
        def _():
            head_sent(hh)
            send_head(hh + AHEAD)
        head_here(hh)
        one_head(hh)
        w_steps(hh)

        @pl.when(hh > 0)
        def _():
            pass_on(hh - 1, 0)
        return carry
    lax.fori_loop(0, LOCAL_HEADS, heads, 0)
    w_steps(LOCAL_HEADS)
    pass_on(LOCAL_HEADS - 1, 0)

    def attended_wait(hh, carry):
        got(at.at[feats(zl, hh), theirs], aor.at[hh])
        got(at.at[feats(1 - zl, hh), theirs], afr.at[hh])
        return carry
    lax.fori_loop(0, LOCAL_HEADS, attended_wait, 0)

    def pair_share(hh, carry):
        got(at.at[feats(zl, hh), pair_mine], por.at[hh])
        pair_share_copy(hh, zl).start()
        got(at.at[feats(1 - zl, hh), pair_mine], par.at[hh])
        pair_share_copy(hh, 1 - zl).start()
        return carry

    def pair_wait(hh, carry):
        for which in range(2):
            got(at.at[feats(which, hh), pair_theirs], pfr.at[hh, which])
        return carry

    def past(i, k):
        return jnp.where(i >= k, 1, 0)

    def slot_of(i):
        return past(i, 2) - past(i, 4) + past(i, 5) - past(i, 7)

    def group_p(i):
        return past(i, 1) - past(i, 2) + past(i, 3) + past(i, 4) + past(i, 6)

    def group_of(i):
        return zh_of(group_p(i))

    def zh_of(p):
        is1 = (p % 2) * (1 - p // 2)
        is2 = (1 - p % 2) * (p // 2)
        is3 = (p % 2) * (p // 2)
        return (zh + 4 - sgn * is1 + sgn * is2 + 2 * is3) % 4

    def lane_block(xx):
        return pl.ds(al(xx * 128, 128), 128)

    def far_copies(i):
        yield rc(far_out.at[i, pl.ds(0, WC), :], far_in.at[i, 0], ffs.at[i, 0], ffr.at[i, 0],
                 dev(xp, y, z, c))
        yield rc(far_out.at[i, pl.ds(WC, WC), :], far_in.at[i, 1], ffs.at[i, 1], ffr.at[i, 1],
                 dev(xm, y, z, c))

    def near_copies(i):
        yield rc(near_out.at[i, 0], near_in.at[i, 0], nns.at[i, 0], nnr.at[i, 0], dev(xp, y, z, c))
        yield rc(near_out.at[i, 1], near_in.at[i, 1], nns.at[i, 1], nnr.at[i, 1], dev(xm, y, z, c))

    def stage_a(i):
        rows = pl.ds(al(group_of(i) * GC, 32), GC)
        lanes = pl.ds(al(slot_of(i) * 512, 128), 512)
        pf[i] = jnp.dot(wt[rows, :], at[:, lanes], preferred_element_type=F32)
        far_out[i] = pf[i, :, lane_block((x + 2) % NX)].astype(BF)
        for cp in far_copies(i):
            cp.start()

    def stage_b(i):
        for d in range(2):
            got(far_in.at[i, d], ffr.at[i, d])
        up = lane_block(xp)
        down = lane_block(xm)
        lo, hi = pl.ds(0, WC), pl.ds(WC, WC)
        near_out[i, 0, lo, :] = (pf[i, lo, up] + far_in[i, 0].astype(F32)).astype(BF)
        near_out[i, 0, hi, :] = pf[i, hi, up].astype(BF)
        near_out[i, 1, lo, :] = pf[i, lo, down].astype(BF)
        near_out[i, 1, hi, :] = (pf[i, hi, down] + far_in[i, 1].astype(F32)).astype(BF)
        for cp in near_copies(i):
            cp.start()

    def stage_c(i):
        for d in range(2):
            got(near_in.at[i, d], nnr.at[i, d])
        rows = pl.ds(al(group_of(i) * GC, 32), GC)
        total = (pf[i, :, lane_block(x)] + near_in[i, 0].astype(F32)
                 + near_in[i, 1].astype(F32))
        whose = slot_of(i)

        @pl.when(whose == 0)
        def _():
            ft[rows, :] = total

        @pl.when(whose == 1)
        def _():
            pair_out[rows, :] = (total * gate_col[rows, :]).astype(BF)
            pair_sum(group_p(i)).start()

    def pair_sum(p):
        rows = pl.ds(al(zh_of(p) * GC, 32), GC)
        return rc(pair_out.at[rows, :], pair_in.at[rows, :], pss.at[p], psr.at[p], pair)

    def inputs_sent():
        for hh in range(LOCAL_HEADS - AHEAD, LOCAL_HEADS):
            head_sent(hh)

        def head_passed(hh, carry):
            @pl.when(jnp.logical_not(q_stays))
            def _():
                q_copy(head, hh, qos.at[hh]).wait_send()
            kv_pass(hh).wait_send()
            return carry
        lax.fori_loop(0, LOCAL_HEADS, head_passed, 0)

        def heads_sent(hh, carry):
            away_copy(hh).wait_send()
            home_copy(hh).wait_send()
            pass_copy(hh).wait_send()
            pair_home_copy(hh).wait_send()
            pair_pass_copy(hh).wait_send()
            for which in range(2):
                pair_share_copy(hh, which).wait_send()
            return carry
        lax.fori_loop(0, LOCAL_HEADS, heads_sent, 0)

    def weights_sent():
        @pl.when(jnp.logical_not(is_row_core))
        def _():
            rc(w_own, piece(z, c), w0s, w0r.at[c], other).wait_send()

        @pl.when(is_row_core)
        def _():
            for d in range(2):
                for k in range(1, 4):
                    z_send(d, k).wait_send()

                @pl.when(d == 1 - zl)
                def _(d=d):
                    z_send(d, 4).wait_send()
            row_send(z, 0).wait_send()
            for k in range(1, 4):
                for d in range(2):
                    row_send(z_from(d, k), z_index(d, k)).wait_send()
            row_send((z + 4) % NZ, 7).wait_send()

    def sums_sent(i):
        for cp in far_copies(i):
            cp.wait_send()
        for cp in near_copies(i):
            cp.wait_send()

    def step(i, carry):
        for p, when in enumerate((0, 1, 4, 6)):
            @pl.when(i == when)
            def _(p=p):
                row_wait(p)

        @pl.when(i == 1)
        def _():
            lax.fori_loop(0, LOCAL_HEADS, pair_share, 0)

        @pl.when(i == 2)
        def _():
            lax.fori_loop(0, LOCAL_HEADS, pair_wait, 0)

        @pl.when(i < GROUPS)
        def _():
            stage_a(i)

        @pl.when(jnp.logical_and(i >= NEAR_LAG, i < GROUPS + NEAR_LAG))
        def _():
            stage_b(i - NEAR_LAG)

        @pl.when(i >= LAST_LAG)
        def _():
            stage_c(i - LAST_LAG)
        w_steps(i, 10)

        @pl.when(i == 5)
        def _():
            inputs_sent()

        @pl.when(i == GROUPS + LAST_LAG - 2)
        def _():
            weights_sent()

        @pl.when(i >= LAST_LAG + 1)
        def _():
            sums_sent(i - LAST_LAG - 1)
        return carry
    def tokens(which, cc):
        return ob.at[which, pl.ds(al(cc * TOK, TOK), TOK), :]

    def out_cols(row):
        return out_hbm.at[0, :, pl.ds(al(row * 1280, 128), 1280)]

    keep = [pltpu.make_async_copy(tokens(i, c), out_cols(row), fink.at[i])
            for i, row in enumerate((my_row, pair_row))]
    give = [rc(tokens(i, oc), out_cols(row), fins.at[i], finr.at[i], other)
            for i, row in enumerate((my_row, pair_row))]
    lax.fori_loop(0, GROUPS + LAST_LAG - 1, step, 0)
    near_half = zh // 2

    def finish_own(half):
        for b in range(5):
            here = pl.ds(al((half * 5 + b) * 128, 128), 128)
            ob[0, :, here] = (ft[here, :].T * gate_row[0, :, here]).astype(BF)

    def finish_pair(half):
        for b in range(5):
            here = pl.ds(al((half * 5 + b) * 128, 128), 128)
            ob[1, :, here] = pair_in[here, :].T

    def pair_here(p):
        got(pair_in.at[pl.ds(al(zh_of(p) * GC, 32), GC), :], psr.at[p])

    finish_own(near_half)
    for p in range(3):
        pair_here(p)
    finish_pair(near_half)
    stage_c(GROUPS - 1)
    finish_own(1 - near_half)
    keep[0].start()
    give[0].start()
    pair_here(3)
    finish_pair(1 - near_half)
    keep[1].start()
    give[1].start()

    for i in range(GROUPS - 2, GROUPS):
        sums_sent(i)
    gate_copy.wait_send()
    for p in range(4):
        pair_sum(p).wait_send()
    for i, yy in enumerate((y, y_pair)):
        keep[i].wait()
        give[i].wait_send()
        differs = (oc - yy % 2) * (oc - yy % 2)
        got(out_cols((1 - differs) * yy + differs * (3 - yy)), finr.at[i])


def body(query_rows, key_rows, value_rows, query_gain, key_gain, out_weight, gate_table, lengths,
         step_index):
    smem = pl.BlockSpec(memory_space=pltpu.SMEM)
    hbm = pl.BlockSpec(memory_space=pl.ANY)
    sem = pltpu.SemaphoreType.DMA
    flops = 2 * (2 * 5 * 512 * 1024 * 128 + 512 * 1280 * 2560)
    return pl.pallas_call(
        kernel,
        out_shape=jax.ShapeDtypeStruct((1, TOK, D), BF),
        in_specs=[smem, smem] + [hbm] * 7,
        out_specs=hbm,
        scratch_shapes=[
            pltpu.VMEM((1, D), F32),
            pltpu.VMEM((1, D), F32),
            pltpu.VMEM((TOK, D), BF),
            pltpu.VMEM((TOK, D), BF),
            pltpu.VMEM((TOK, D), BF),
            pltpu.VMEM((TOK, D), BF),
            pltpu.VMEM((TOK, 2 * D), BF),
            pltpu.VMEM((WC, GW), BF),
            pltpu.VMEM((2, STEPS, 1280), F32),
            pltpu.VMEM((3, 1, 1280), F32),
            pltpu.VMEM((512, GW), BF),
            pltpu.VMEM((KEYS, 2 * GW), BF),
            pltpu.VMEM((KEYS, 128), F32),
            pltpu.VMEM((1280, 2 * GW), BF),
            pltpu.VMEM((LOCAL_HEADS, HD, 256), BF),
            pltpu.VMEM((2 * GW, 1024), BF),
            pltpu.VMEM((GROUPS, GC, 512), F32),
            pltpu.VMEM((GROUPS, GC, 128), BF),
            pltpu.VMEM((GROUPS, 2, WC, 128), BF),
            pltpu.VMEM((GROUPS, 2, GC, 128), BF),
            pltpu.VMEM((GROUPS, 2, GC, 128), BF),
            pltpu.VMEM((1280, 128), F32),
            pltpu.VMEM((1280, 128), F32),
            pltpu.VMEM((1280, 128), BF),
            pltpu.VMEM((1280, 128), BF),
            pltpu.VMEM((2, 128, 1280), BF),
            sem((8,)),
            sem, sem,
            sem((5,)), sem((5,)), sem((5,)), sem((5,)), sem((5,)),
            sem((5,)), sem((5,)),
            sem, sem((2,)),
            sem((2, 4)), sem((2, 4)),
            sem((8,)), sem((8,)),
            sem((5,)), sem((5,)), sem((5,)), sem((5,)), sem((5,)), sem((5,)),
            sem((5,)), sem((5,)), sem((5,)), sem((5,)), sem((5, 2)), sem((5, 2)),
            sem((8, 2)), sem((8, 2)), sem((8, 2)), sem((8, 2)),
            sem((4,)), sem((4,)),
            sem((2,)), sem((2,)), sem((2,)),
        ],
        compiler_params=pltpu.CompilerParams(
            collective_id=0, has_side_effects=True, vmem_limit_bytes=60 * 2**20),
        cost_estimate=pl.CostEstimate(flops=flops, bytes_accessed=4 * 2**20,
                                      transcendentals=5 * 512 * 1024),
        name="gated_attention",
    )(lengths, step_index, query_rows, key_rows, value_rows, query_gain[None], key_gain[None],
      out_weight.T, gate_table)


def solution(mesh):
    placed = (
        P("slot", ("head", "blk"), None),
        P("slot", ("head", "blk"), None),
        P("slot", ("head", "blk"), None),
        P(),
        P(),
        P("head", ("slot", "blk")),
        P(),
        P("slot"),
        P("slot"),
    )
    return jax.shard_map(
        body,
        mesh=mesh,
        in_specs=placed,
        out_specs=P("slot", ("head", "blk"), None),
        check_vma=False,
    )
```
